32 devices in a mesh: section: 4 (over x, core), fsdp: 8 (over z, y).
Axes of the slice: x: 2, y: 2, z: 4, core: 2. Of those that a mesh axis runs over, the one named last changes fastest.
Arguments:
- activations: bfloat16 [4, 1024, 4096], P('section', 'fsdp'), may hold values from -6 to 6
- norm_gain: float32 [4, 4096], P('section'), may hold values from 0.1 to 1.9
- trunk_weight: bfloat16 [4, 4096, 4096], P('section', 'fsdp'), may hold values from -0.09375 to 0.09375
- head_weight: bfloat16 [4, 4096, 128], P(None, 'fsdp'), may hold values from -0.09375 to 0.09375
- head_mix: float32 [4, 128, 128], replicated, may hold values from -0.5 to 0.5
- head_steps: int32 [4], replicated, may hold values from 0 to 3, each once
- task_of: int32 [8, 1], replicated, may hold values from 0 to 3
- loss_ratio: float32 [4], replicated, may hold values from 0.5 to 2
- targets: bfloat16 [1024, 128], P('fsdp'), may hold values from -6 to 6
Outputs:
- passed: bfloat16 [4, 1024, 4096], P('section', 'fsdp')
- joined_grad: float32 [4096, 4096], P('fsdp', 'section')
- task_weights: float32 [4], replicated
- task_losses: float32 [4], replicated
The draws below stay inside these ranges and needn't reach their ends.
Inputs may be any that keep to these rules, and one draw needn't show every extreme that they name: `head_steps`: each value appears once. `task_of`: every task is named by at least one block.
All inputs are finite; a program needn't handle non-finite values.
Results may differ from the reference program's by a relative error of at most 0.017.
Values may be sent and summed in bfloat16 or wider, within the bound.
A program may use at most 64 MiB of HBM per device.

```python
import math
import jax
import jax.numpy as jnp
from jax import lax

DW = 4096
TOK_DEV = 128
TASKS = 4
OUTS = 128
TOKENS = 1024
N_SECTION = 4
N_FSDP = 8


def block_scale(stream_key, dims, split, smallest, largest):
    def one(position, blocks):
        draws = jax.random.uniform(jax.random.fold_in(jax.random.fold_in(stream_key, 6), position), (blocks,), jnp.float32, smallest / len(split), largest / len(split))
        return jnp.repeat(jnp.exp(draws), dims[position] // blocks).reshape((-1,) + (1,) * (len(dims) - position - 1))

    factor_of = one(*split[0])
    for cut in split[1:]:
        factor_of = factor_of * one(*cut)
    return factor_of


def choose_distinct(key, rows, amount, top, lift):
    ranking = jax.random.permutation(jax.random.fold_in(key, 1), amount)
    boost = ranking
    for power in range(3):
        boost = boost * boost // amount
    boost = boost * lift // amount
    chance = jax.random.randint(jax.random.fold_in(key, 2), (rows, amount), 0, 4096) + boost
    holders = jax.random.permutation(jax.random.fold_in(key, 3), rows)[jnp.arange(amount) % rows]
    chance = jnp.where(jnp.arange(rows)[:, None] == holders[None, :], 1 << 14, chance)
    priority = chance * amount + jnp.arange(amount)
    return lax.top_k(priority.astype(jnp.int32), top)[1].astype(jnp.int32)


def bell_draw(key, shape, spread, limit, cuts=(), kind=jnp.bfloat16):
    factor_of = block_scale(key, shape, cuts, -0.22, 0.18) if cuts else 1.0
    entries = jax.random.normal(key, shape, jnp.float32) * spread * factor_of
    return jnp.minimum(jnp.maximum(entries, -limit), limit).astype(kind)


def setup_inputs(seed: int = 0) -> dict:
    keys = jax.random.split(jax.random.key(seed), 10)
    activations = bell_draw(keys[0], (N_SECTION, TOKENS, DW), 1.0, 6.0, ((0, 4), (1, 8)))
    norm_gain = jnp.clip(1.0 + 0.18 * jax.random.normal(keys[1], (N_SECTION, DW), jnp.float32), 0.1, 1.9)
    trunk_weight = bell_draw(keys[2], (N_SECTION, DW, DW), DW ** -0.5, 0.09375, ((0, 4), (1, 8)))
    head_weight = bell_draw(keys[3], (TASKS, DW, OUTS), DW ** -0.5, 0.09375, ((1, 8),))
    head_mix = bell_draw(keys[4], (TASKS, OUTS, OUTS), OUTS ** -0.5, 0.5, (), jnp.float32)
    head_steps = jax.random.permutation(keys[5], TASKS).astype(jnp.int32)
    task_of = choose_distinct(keys[6], N_FSDP, TASKS, 1, 2048)
    loss_ratio = jnp.clip(jnp.exp(jax.random.uniform(keys[7], (TASKS,), jnp.float32, math.log(0.5), math.log(2.0))), 0.5, 2.0)
    targets = bell_draw(keys[8], (TOKENS, OUTS), 1.0, 6.0, ((0, 8),))
    return dict(activations=activations, norm_gain=norm_gain, trunk_weight=trunk_weight, head_weight=head_weight, head_mix=head_mix, head_steps=head_steps, task_of=task_of, loss_ratio=loss_ratio, targets=targets)


EPS = 1e-05
ALPHA = 1.5

def rms_scale(values):
    return values * lax.rsqrt(lax.optimization_barrier(jnp.mean(values * values, axis=-1, keepdims=True)) + EPS)

def section_layer(hidden, gain, weight):
    normed = (rms_scale(hidden.astype(jnp.float32)) * gain).astype(jnp.bfloat16)
    pre = jnp.dot(normed, weight, preferred_element_type=jnp.float32).astype(jnp.bfloat16)
    output = (hidden.astype(jnp.float32) + jax.nn.silu(pre.astype(jnp.float32))).astype(jnp.bfloat16)
    return (normed, pre, output)

def head_loss(blocks, head_w, mix_w, step_total, target):
    head_in = rms_scale(blocks).astype(jnp.bfloat16)
    outputs = jnp.dot(head_in, head_w, preferred_element_type=jnp.float32)
    for depth_index in range(TASKS):
        active = (depth_index < step_total).astype(jnp.float32)
        outputs = outputs + active * jnp.tanh(jnp.dot(outputs, mix_w, precision=lax.Precision.HIGHEST))
    error_term = outputs - target.astype(jnp.float32)
    return 0.5 * jnp.sum(error_term * error_term)

def reference(activations, norm_gain, trunk_weight, head_weight, head_mix, head_steps, task_of, loss_ratio, targets):
    section_outs = lax.map(lambda section_args: section_layer(section_args[0], section_args[1], section_args[2])[2], (activations, norm_gain, trunk_weight))
    passed = jnp.concatenate([jnp.zeros((1, TOKENS, DW), jnp.bfloat16), section_outs[:-1]], axis=0)
    last_section = N_SECTION - 1
    normed_last, pre_last, out_last = section_layer(activations[last_section], norm_gain[last_section], trunk_weight[last_section])
    block_rows = out_last.astype(jnp.float32).reshape(N_FSDP, TOK_DEV, DW)
    task_ids = task_of[:, 0]
    target_blocks = targets.reshape(N_FSDP, TOK_DEV, OUTS)

    def per_block(block_args):
        blocks, task_id, target = block_args
        loss_value, pullback = jax.vjp(lambda inner: head_loss(inner, head_weight[task_id], head_mix[task_id], head_steps[task_id] + 1, target), blocks)
        return (loss_value, pullback(jnp.ones_like(loss_value))[0])
    block_losses, grad_out = lax.map(per_block, (block_rows, task_ids, target_blocks))
    onehot = (task_ids[:, None] == jnp.arange(TASKS)[None, :]).astype(jnp.float32)
    counts = TOK_DEV * lax.optimization_barrier(jnp.sum(onehot, axis=0))
    task_losses = lax.optimization_barrier(jnp.sum(onehot * block_losses[:, None], axis=0)) / (counts * OUTS)
    squares = lax.optimization_barrier(jnp.sum(grad_out * grad_out, axis=(1, 2)))
    grad_norms = jnp.sqrt(lax.optimization_barrier(jnp.sum(onehot * squares[:, None], axis=0)))
    target_norms = jnp.mean(grad_norms) * loss_ratio ** ALPHA
    ratios = target_norms / grad_norms
    task_weights = TASKS * ratios / jnp.sum(ratios)
    pre_float = pre_last.astype(jnp.float32)
    sigmoid_pre = jax.nn.sigmoid(pre_float)
    slope_term = sigmoid_pre * (1.0 + pre_float * (1.0 - sigmoid_pre))
    cotangent = (grad_out.reshape(TOKENS, DW) * slope_term).astype(jnp.bfloat16)
    row_weight = jnp.repeat(task_weights[task_ids], TOK_DEV)
    joined_grad = jnp.dot(normed_last.astype(jnp.float32).T, cotangent.astype(jnp.float32) * row_weight[:, None], precision=lax.Precision.HIGHEST)
    return (passed, joined_grad, task_weights, task_losses)
```

```python
import jax
import jax.numpy as jnp
from jax import lax
from jax.sharding import PartitionSpec as P

EPS = 1e-05
ALPHA = 1.5
BF = jnp.bfloat16
F32 = jnp.float32


def rms_scale(values):
    return values * lax.rsqrt(jnp.mean(values * values, axis=-1, keepdims=True) + EPS)


def head_loss(blocks, head_w, mix_w, step_total, target, tasks):
    head_in = rms_scale(blocks).astype(BF)
    outputs = jnp.dot(head_in, head_w, preferred_element_type=F32)
    for depth_index in range(tasks):
        active = (depth_index < step_total).astype(F32)
        outputs = outputs + active * jnp.tanh(
            jnp.dot(outputs, mix_w, precision=lax.Precision.HIGHEST)
        )
    error_term = outputs - target.astype(F32)
    return 0.5 * jnp.sum(error_term * error_term)


def line_reduce_scatter(blocks, place, count, inner, stride):
    if count == 1:
        return blocks[0].astype(F32)
    devices = lax.axis_size("fsdp")

    def pairs(step, limit):
        found = []
        for index in range(devices):
            spot = index // stride % count
            if 0 <= spot + step < count and limit(spot):
                found.append((index, index + step * stride))
        return found

    def pick(position):
        return lax.dynamic_index_in_dim(blocks, jnp.clip(position, 0, count - 1), 0, keepdims=False)

    own = pick(place).astype(F32)
    if count == 2:
        swap = pairs(1, lambda s: True) + pairs(-1, lambda s: True)
        return own + lax.ppermute(pick(1 - place).astype(BF), "fsdp", swap).astype(F32)
    right = left = None
    for t in range(1, count):
        send_right = pick(count - t + place)
        send_left = pick(place - count + t)
        if right is not None:
            send_right = send_right.astype(F32) + right.astype(F32)
            send_left = send_left.astype(F32) + left.astype(F32)
        right = lax.ppermute(send_right.astype(BF), "fsdp", pairs(1, lambda s: s <= t - 1))
        left = lax.ppermute(send_left.astype(BF), "fsdp", pairs(-1, lambda s: s >= count - t))
    return own + right.astype(F32) + left.astype(F32)


def spread_pairs(size, bit):
    low = (1 << (bit + 1)) - 1
    return [(i, i ^ (1 << bit)) for i in range(size) if i & low == low]


def local(
    activations,
    norm_gain,
    trunk_weight,
    head_weight,
    head_mix,
    head_steps,
    task_of,
    loss_ratio,
    targets,
):
    fsdp_size = lax.axis_size("fsdp")
    section_size = lax.axis_size("section")
    member = lax.axis_index("fsdp")
    section_index = lax.axis_index("section")
    last_section = section_size - 1
    is_last = section_index == last_section
    section_bits = section_size.bit_length() - 1
    y_size = 1 << ((fsdp_size.bit_length() - 1) // 2)
    z_size = fsdp_size // y_size
    y_place = member % y_size
    z_place = member // y_size
    tasks, head_rows, outs = head_weight.shape

    hidden = activations[0]
    rows, features = hidden.shape
    normed = (rms_scale(hidden.astype(F32)) * norm_gain[0]).astype(BF)
    feature_block = lax.all_to_all(normed, "fsdp", split_axis=1, concat_axis=0, tiled=True)
    weight = trunk_weight[0]

    wanted = head_weight[task_of[:, 0]]
    if head_rows % section_size == 0 and (head_rows // section_size) % 16 == 0:
        share = head_rows // section_size
        part = lax.dynamic_slice_in_dim(wanted, section_index * share, share, 1)
        part = lax.all_to_all(part, "fsdp", split_axis=0, concat_axis=0, tiled=True)
        part = lax.all_gather(part, "section", axis=1, tiled=True)
    else:
        part = lax.all_to_all(wanted, "fsdp", split_axis=0, concat_axis=0, tiled=True)
    head_w = part.reshape(features, outs)

    chunks = 4
    width = features // chunks
    pieces = []
    for c in range(chunks):
        partial = jnp.dot(
            feature_block, weight[:, c * width : (c + 1) * width], preferred_element_type=F32
        ).astype(BF)
        partial = partial.reshape(z_size, y_size, rows, width)
        if c == 1:
            partial = line_reduce_scatter(partial, z_place, z_size, y_size, y_size)
            total = line_reduce_scatter(partial, y_place, y_size, 1, 1)
        else:
            partial = line_reduce_scatter(partial.swapaxes(0, 1), y_place, y_size, 1, 1)
            total = line_reduce_scatter(partial, z_place, z_size, y_size, y_size)
        pieces.append(total.astype(BF))
    pre = jnp.concatenate(pieces, axis=1)
    output = (hidden.astype(F32) + jax.nn.silu(pre.astype(F32))).astype(BF)
    passed = lax.ppermute(output, "section", [(i, i + 1) for i in range(section_size - 1)])

    feature_all = feature_block
    for bit in reversed(range(section_bits)):
        got = lax.ppermute(feature_all, "section", spread_pairs(section_size, bit))
        takes = (section_index >> bit & 1 == 0) & (
            section_index & ((1 << bit) - 1) == (1 << bit) - 1
        )
        feature_all = jnp.where(takes, got, feature_all)

    task_id = task_of[member, 0]
    onehot = (task_of[:, 0][:, None] == jnp.arange(tasks)[None, :]).astype(F32)
    counts = rows * jnp.sum(onehot, axis=0)
    own_task = (jnp.arange(tasks) == task_id).astype(F32)
    block_loss, pullback = jax.vjp(
        lambda inner: head_loss(
            inner, head_w, head_mix[task_id], head_steps[task_id] + 1, targets, tasks
        ),
        output.astype(F32),
    )
    grad_out = pullback(jnp.ones_like(block_loss))[0]
    square = jnp.sum(grad_out * grad_out)
    pre_float = pre.astype(F32)
    sigmoid_pre = jax.nn.sigmoid(pre_float)
    slope_term = sigmoid_pre * (1.0 + pre_float * (1.0 - sigmoid_pre))
    cotangent = (grad_out * slope_term).astype(BF)

    col_width = features // section_size
    cols = cotangent.reshape(rows, section_size, col_width)
    for bit in reversed(range(section_bits)):
        half = cols.reshape(rows, 2, cols.shape[1] // 2, col_width)
        low, high = half[:, 0], half[:, 1]
        got = lax.ppermute(low, "section", spread_pairs(section_size, bit))
        cols = jnp.where(section_index >> bit & 1 == 0, got, high)
    column_block = lax.all_gather(cols[:, 0], "fsdp", axis=0, tiled=True)

    sums = jnp.concatenate([own_task * square, own_task * block_loss])
    sums = lax.psum(jnp.where(is_last, sums, jnp.zeros_like(sums)), ("section", "fsdp"))
    norm_sums, loss_sums = sums[:tasks], sums[tasks:]
    grad_norms = jnp.sqrt(norm_sums)
    ratios = jnp.mean(grad_norms) * loss_ratio**ALPHA / grad_norms
    task_weights = tasks * ratios / jnp.sum(ratios)
    task_losses = loss_sums / (counts * outs)

    block_weight = jnp.sum(onehot * task_weights[None, :], axis=1)
    scaled = (
        column_block.reshape(fsdp_size, rows, col_width).astype(F32)
        * block_weight[:, None, None]
    ).astype(BF)
    joined_grad = lax.dot_general(
        feature_all,
        scaled.reshape(fsdp_size * rows, col_width),
        (((0,), (0,)), ((), ())),
        preferred_element_type=F32,
    )
    return (passed[None], joined_grad, task_weights, task_losses)


def solution(mesh):
    return jax.shard_map(
        local,
        mesh=mesh,
        in_specs=(
            P("section", "fsdp", None),
            P("section", None),
            P("section", "fsdp", None),
            P(None, "fsdp", None),
            P(),
            P(),
            P(),
            P(),
            P("fsdp", None),
        ),
        out_specs=(P("section", "fsdp", None), P("fsdp", "section"), P(), P()),
        check_vma=False,
    )
```

```python
import functools

import jax
import jax.numpy as jnp
from jax import lax
from jax.experimental import pallas as pl
from jax.experimental.pallas import tpu as pltpu
from jax.sharding import PartitionSpec as P

EPS = 1e-05
ALPHA = 1.5
BF = jnp.bfloat16
F32 = jnp.float32
MESH = pl.DeviceIdType.MESH
CHUNKS = 8
HALVES = 2
VMEM_MAX = 48 << 20


def rms_scale(values):
    return values * lax.rsqrt(jnp.mean(values * values, axis=-1, keepdims=True) + EPS)


def head_loss(blocks, head_w, mix_w, step_total, target, tasks):
    head_in = rms_scale(blocks).astype(BF)
    outputs = jnp.dot(head_in, head_w, preferred_element_type=F32)
    for depth_index in range(tasks):
        active = (depth_index < step_total).astype(F32)
        outputs = outputs + active * jnp.tanh(
            jnp.dot(outputs, mix_w, precision=lax.Precision.HIGHEST)
        )
    error_term = outputs - target.astype(F32)
    return 0.5 * jnp.sum(error_term * error_term)


def line_reduce_scatter(blocks, place, count, inner, stride):
    if count == 1:
        return blocks[0].astype(F32)
    devices = lax.axis_size("fsdp")

    def pairs(step, limit):
        found = []
        for index in range(devices):
            spot = index // stride % count
            if 0 <= spot + step < count and limit(spot):
                found.append((index, index + step * stride))
        return found

    def pick(position):
        return lax.dynamic_index_in_dim(blocks, jnp.clip(position, 0, count - 1), 0, keepdims=False)

    own = pick(place).astype(F32)
    if count == 2:
        swap = pairs(1, lambda s: True) + pairs(-1, lambda s: True)
        return own + lax.ppermute(pick(1 - place).astype(BF), "fsdp", swap).astype(F32)
    right = left = None
    for t in range(1, count):
        send_right = pick(count - t + place)
        send_left = pick(place - count + t)
        if right is not None:
            send_right = send_right.astype(F32) + right.astype(F32)
            send_left = send_left.astype(F32) + left.astype(F32)
        right = lax.ppermute(send_right.astype(BF), "fsdp", pairs(1, lambda s: s <= t - 1))
        left = lax.ppermute(send_left.astype(BF), "fsdp", pairs(-1, lambda s: s >= count - t))
    return own + right.astype(F32) + left.astype(F32)


def spread_pairs(size, bit):
    low = (1 << (bit + 1)) - 1
    return [(i, i ^ (1 << bit)) for i in range(size) if i & low == low]


def remote(src, dst, send, recv, **place):
    return pltpu.make_async_remote_copy(
        src_ref=src, dst_ref=dst, send_sem=send, recv_sem=recv, device_id=place,
        device_id_type=MESH,
    )


def greet(fsdp, sections):
    me, section = lax.axis_index("fsdp"), lax.axis_index("section")
    barrier = pltpu.get_barrier_semaphore()
    for j in range(1, fsdp):
        pl.semaphore_signal(
            barrier, inc=1, device_id={"fsdp": lax.rem(me + j, fsdp)}, device_id_type=MESH
        )
    for j in range(1, sections):
        pl.semaphore_signal(
            barrier, inc=1, device_id={"section": lax.rem(section + j, sections)},
            device_id_type=MESH,
        )
    pl.semaphore_wait(barrier, fsdp + sections - 2)


def project_kernel(
    fsdp, sections, planes, chunks,
    hidden, gain, weight, pre, feat,
    normed, tokens, part, y_in, z_in, z_in0,
    tok_send, tok_recv, y_send, y_recv, z_send, z_recv, f_send, f_recv,
):
    me, section = lax.axis_index("fsdp"), lax.axis_index("section")
    y, z = lax.rem(me, 2), me // 2
    rows, features = hidden.shape
    depth = features // fsdp
    width = features // chunks
    last = sections - 1
    greet(fsdp, sections)

    @pl.loop(0, rows // 16)
    def _(i):
        r = pl.ds(pl.multiple_of(i * 16, 16), 16)
        normed[r, :] = (rms_scale(hidden[r, :].astype(F32)) * gain[...]).astype(BF)

    def token_copy(j):
        to = lax.rem(me + j, fsdp)
        return remote(
            normed.at[:, pl.ds(pl.multiple_of(to * depth, 128), depth)], tokens.at[y, z],
            tok_send.at[j - 1], tok_recv.at[j - 1], fsdp=to,
        )

    for j in range(1, fsdp):
        token_copy(j).start()
    tokens[y, z] = normed[:, pl.ds(pl.multiple_of(me * depth, 128), depth)]
    for j in range(1, fsdp):
        token_copy(j).wait_recv()

    def feature_copy(to):
        return remote(tokens, feat, f_send.at[to], f_recv, section=to)

    @pl.when(section == last)
    def _():
        for to in range(last):
            feature_copy(to).start()
        feat[...] = tokens[...]

    def y_copy(c):
        return remote(
            part.at[c, 1 - y], y_in.at[c], y_send.at[c], y_recv.at[c], fsdp=z * 2 + 1 - y
        )

    def y_copy0():
        return remote(
            part.at[0, 1 - y, z], y_in.at[0, 0], y_send.at[0], y_recv.at[0], fsdp=z * 2 + 1 - y
        )

    def z_copy(c, way, t):
        d = planes - t + z if way == 0 else z - planes + t
        d = jnp.minimum(jnp.maximum(d, 0), planes - 1)
        to = jnp.minimum(z + 1, planes - 1) if way == 0 else jnp.maximum(z - 1, 0)
        if isinstance(c, int):
            src, dst = part.at[0, :, d], z_in0.at[way, t - 1]
        else:
            src, dst = part.at[c, y, d], z_in.at[c, way, t - 1]
        return d, remote(
            src, dst, z_send.at[c, way, t - 1], z_recv.at[c, way, t - 1], fsdp=to * 2 + y
        )

    def sends(way, t):
        if way == 0:
            return (z <= t - 1) & (z < planes - 1)
        return (z >= planes - t) & (z > 0)

    def receives(way, t):
        if way == 0:
            return (z >= 1) & (z <= t)
        return (z <= planes - 2) & (z >= planes - 1 - t)

    def z_start(c, t):
        for way in range(2):
            d, copy = z_copy(c, way, t)
            if t > 1:

                @pl.when(sends(way, t) & receives(way, t - 1))
                def _():
                    z_copy(c, way, t - 1)[1].wait_recv()
                    if isinstance(c, int):
                        for k in range(2):
                            part[0, k, d] = (
                                part[0, k, d].astype(F32) + z_in0[way, t - 2, k].astype(F32)
                            ).astype(BF)
                    else:
                        part[c, y, d] = (
                            part[c, y, d].astype(F32) + z_in[c, way, t - 2].astype(F32)
                        ).astype(BF)

            @pl.when(sends(way, t))
            def _():
                copy.start()

    def z_last(c):
        t = planes - 1
        for way in range(2):

            @pl.when(receives(way, t))
            def _():
                z_copy(c, way, t)[1].wait_recv()
                if isinstance(c, int):
                    for k in range(2):
                        part[0, k, z] = (
                            part[0, k, z].astype(F32) + z_in0[way, t - 1, k].astype(F32)
                        ).astype(BF)
                else:
                    part[c, y, z] = (
                        part[c, y, z].astype(F32) + z_in[c, way, t - 1].astype(F32)
                    ).astype(BF)

    ahead = min(3, chunks - 1)

    @pl.loop(0, chunks)
    def _(c):
        block = weight[:, pl.ds(pl.multiple_of(c * width, 128), width)]
        for k in range(2):
            part[c, k] = (
                jnp.dot(
                    tokens[k].reshape(planes * rows, depth), block, preferred_element_type=F32
                )
                .astype(BF)
                .reshape(planes, rows, width)
            )

        @pl.when(c == 0)
        def _():
            z_start(0, 1)

        @pl.when((c >= 1) & (c <= ahead))
        def _():
            y_copy(c).start()

    @pl.loop(1, chunks + planes - 1)
    def _(i):
        for t in range(1, planes):

            @pl.when(i == t)
            def _():
                if t < planes - 1:
                    z_start(0, t + 1)
                else:
                    z_last(0)
                    y_copy0().start()

        @pl.when(i < chunks)
        def _():
            y_copy(i).wait_recv()

            @pl.when(i + ahead < chunks)
            def _():
                y_copy(i + ahead).start()

            for d in range(planes):
                part[i, y, d] = (part[i, y, d].astype(F32) + y_in[i, d].astype(F32)).astype(BF)
            z_start(i, 1)

        for t in range(1, planes - 1):
            c = i - t

            @pl.when((c >= 1) & (c < chunks))
            def _():
                z_start(c, t + 1)

        c = i - (planes - 1)

        @pl.when((c >= 1) & (c < chunks))
        def _():
            z_last(c)
            pre[:, pl.ds(pl.multiple_of(c * width, 128), width)] = part[c, y, z]

    y_copy0().wait_recv()
    pre[:, pl.ds(0, width)] = (part[0, y, z].astype(F32) + y_in[0, 0].astype(F32)).astype(BF)

    @pl.when(section != last)
    def _():
        feature_copy(0).wait_recv()

    @pl.when(section == last)
    def _():
        for to in range(last):
            feature_copy(to).wait_send()

    for j in range(1, fsdp):
        token_copy(j).wait_send()
    y_copy0().wait_send()
    for t in range(1, planes):
        for way in range(2):

            @pl.when(sends(way, t))
            def _():
                z_copy(0, way, t)[1].wait_send()

    @pl.loop(1, chunks)
    def _(c):
        y_copy(c).wait_send()
        for t in range(1, planes):
            for way in range(2):

                @pl.when(sends(way, t))
                def _():
                    z_copy(c, way, t)[1].wait_send()


def project(hidden, gain, weight, fsdp, sections):
    rows, features = hidden.shape
    planes, chunks = fsdp // 2, CHUNKS
    depth, width = features // fsdp, features // chunks
    dma = pltpu.SemaphoreType.DMA
    vmem = pl.BlockSpec(memory_space=pltpu.VMEM)
    return pl.pallas_call(
        functools.partial(project_kernel, fsdp, sections, planes, chunks),
        out_shape=(
            jax.ShapeDtypeStruct((rows, features), BF),
            jax.ShapeDtypeStruct((2, planes, rows, depth), BF),
        ),
        in_specs=[vmem] * 3,
        out_specs=(vmem, vmem),
        scratch_shapes=[
            pltpu.VMEM((rows, features), BF),
            pltpu.VMEM((2, planes, rows, depth), BF),
            pltpu.VMEM((chunks, 2, planes, rows, width), BF),
            pltpu.VMEM((chunks, planes, rows, width), BF),
            pltpu.VMEM((chunks, 2, planes - 1, rows, width), BF),
            pltpu.VMEM((2, planes - 1, 2, rows, width), BF),
            dma((fsdp - 1,)),
            dma((fsdp - 1,)),
            dma((chunks,)),
            dma((chunks,)),
            dma((chunks, 2, planes - 1)),
            dma((chunks, 2, planes - 1)),
            dma((sections,)),
            dma,
        ],
        compiler_params=pltpu.CompilerParams(
            collective_id=0, has_side_effects=True, vmem_limit_bytes=VMEM_MAX
        ),
        cost_estimate=pl.CostEstimate(
            flops=2 * fsdp * rows * depth * features, bytes_accessed=1 << 23, transcendentals=0
        ),
    )(hidden, gain, weight)


def gather_kernel(
    fsdp, sections, planes,
    cot, stats, cols, table,
    x_send, x_recv, sx_send, sx_recv, st_send, st_recv, z_send, z_recv, y_send, y_recv,
):
    me, section = lax.axis_index("fsdp"), lax.axis_index("section")
    y, z = lax.rem(me, 2), me // 2
    last = sections - 1
    rows, features = cot.shape
    width = features // sections
    size = rows // HALVES
    greet(fsdp, sections)

    def stats_x(to):
        return remote(stats, table.at[y, z], sx_send.at[to], sx_recv, section=to)

    def cols_x(to, h):
        return remote(
            cot.at[pl.ds(h * size, size), pl.ds(to * width, width)], cols.at[y, z, h],
            x_send.at[to, h], x_recv.at[h], section=to,
        )

    def stats_f(j):
        return remote(
            table.at[y, z], table.at[y, z], st_send.at[j - 1], st_recv.at[j - 1],
            fsdp=lax.rem(me + j, fsdp),
        )

    def y_copy(plane, h):
        block = cols.at[y, plane, h]
        return remote(
            block, block, y_send.at[plane, h], y_recv.at[plane, h], fsdp=z * 2 + 1 - y
        )

    def z_copy(way, t, h):
        if way == 0:
            plane, to = jnp.maximum(z - t + 1, 0), jnp.minimum(z + 1, planes - 1)
        else:
            plane, to = jnp.minimum(z + t - 1, planes - 1), jnp.maximum(z - 1, 0)
        block = cols.at[y, plane, h]
        return remote(
            block, block, z_send.at[way, t - 1, h], z_recv.at[way, t - 1, h], fsdp=to * 2 + y
        )

    def sends(way, t):
        if way == 0:
            return (z < planes - 1) & (z - t + 1 >= 0)
        return (z > 0) & (z + t - 1 <= planes - 1)

    def receives(way, t):
        return z - t >= 0 if way == 0 else z + t <= planes - 1

    @pl.when(section == last)
    def _():
        for to in range(last):
            stats_x(to).start()
        for h in range(HALVES):
            for to in range(last):
                cols_x(to, h).start()
        table[y, z] = stats[...]
        for h in range(HALVES):
            cols[y, z, h] = cot[pl.ds(h * size, size), pl.ds(last * width, width)]

    @pl.when(section != last)
    def _():
        stats_x(0).wait_recv()

    for j in range(1, fsdp):
        stats_f(j).start()
    for h in range(HALVES):

        @pl.when(section != last)
        def _():
            cols_x(0, h).wait_recv()

        for way in range(2):

            @pl.when(sends(way, 1))
            def _():
                z_copy(way, 1, h).start()

        y_copy(z, h).start()
    for t in range(1, planes):
        for h in range(HALVES):
            for way in range(2):

                @pl.when(receives(way, t))
                def _():
                    z_copy(way, t, h).wait_recv()
                    y_copy(z - t if way == 0 else z + t, h).start()

                if t < planes - 1:

                    @pl.when(sends(way, t + 1))
                    def _():
                        z_copy(way, t + 1, h).start()

    for j in range(1, fsdp):
        stats_f(j).wait()
    for plane in range(planes):
        for h in range(HALVES):
            y_copy(plane, h).wait()
    for t in range(1, planes):
        for h in range(HALVES):
            for way in range(2):

                @pl.when(sends(way, t))
                def _():
                    z_copy(way, t, h).wait_send()

    @pl.when(section == last)
    def _():
        for to in range(last):
            stats_x(to).wait_send()
            for h in range(HALVES):
                cols_x(to, h).wait_send()


def gather(cot, stats, fsdp, sections):
    rows, features = cot.shape
    planes = fsdp // 2
    width = features // sections
    dma = pltpu.SemaphoreType.DMA
    vmem = pl.BlockSpec(memory_space=pltpu.VMEM)
    return pl.pallas_call(
        functools.partial(gather_kernel, fsdp, sections, planes),
        out_shape=(
            jax.ShapeDtypeStruct((2, planes, HALVES, rows // HALVES, width), BF),
            jax.ShapeDtypeStruct((2, planes) + stats.shape, F32),
        ),
        in_specs=[vmem] * 2,
        out_specs=(vmem, vmem),
        scratch_shapes=[
            dma((sections, HALVES)),
            dma((HALVES,)),
            dma((sections,)),
            dma,
            dma((fsdp - 1,)),
            dma((fsdp - 1,)),
            dma((2, planes - 1, HALVES)),
            dma((2, planes - 1, HALVES)),
            dma((planes, HALVES)),
            dma((planes, HALVES)),
        ],
        compiler_params=pltpu.CompilerParams(
            collective_id=1, has_side_effects=True, vmem_limit_bytes=VMEM_MAX
        ),
        cost_estimate=pl.CostEstimate(flops=0, bytes_accessed=1 << 23, transcendentals=0),
    )(cot, stats)


def kernels_fit(rows, features, fsdp, sections):
    if fsdp < 4 or fsdp % 2 or sections < 2:
        return False
    planes = fsdp // 2
    block = rows * features * 2
    planned = block * (2 * planes + planes + 2 * planes - 2 + 7) + features // fsdp * features * 2
    return (
        planned <= VMEM_MAX * 3 // 4
        and rows % (16 * HALVES) == 0
        and CHUNKS >= planes + 1
        and features % (128 * CHUNKS) == 0
        and features % (128 * fsdp) == 0
        and features % (128 * sections) == 0
        and 1 << ((fsdp.bit_length() - 1) // 2) == 2
    )


def project_permuted(feature_block, weight, rows, y_size, z_size, y_place, z_place):
    features = weight.shape[1]
    chunks = 4
    width = features // chunks
    pieces = []
    for c in range(chunks):
        partial = jnp.dot(
            feature_block, weight[:, c * width : (c + 1) * width], preferred_element_type=F32
        ).astype(BF)
        partial = partial.reshape(z_size, y_size, rows, width)
        if c == 1:
            partial = line_reduce_scatter(partial, z_place, z_size, y_size, y_size)
            total = line_reduce_scatter(partial, y_place, y_size, 1, 1)
        else:
            partial = line_reduce_scatter(partial.swapaxes(0, 1), y_place, y_size, 1, 1)
            total = line_reduce_scatter(partial, z_place, z_size, y_size, y_size)
        pieces.append(total.astype(BF))
    return jnp.concatenate(pieces, axis=1)


def from_last(feature_all, section_index, section_size):
    for bit in reversed(range(section_size.bit_length() - 1)):
        got = lax.ppermute(feature_all, "section", spread_pairs(section_size, bit))
        takes = (section_index >> bit & 1 == 0) & (
            section_index & ((1 << bit) - 1) == (1 << bit) - 1
        )
        feature_all = jnp.where(takes, got, feature_all)
    return feature_all


def local(
    activations,
    norm_gain,
    trunk_weight,
    head_weight,
    head_mix,
    head_steps,
    task_of,
    loss_ratio,
    targets,
):
    fsdp_size = lax.axis_size("fsdp")
    section_size = lax.axis_size("section")
    member = lax.axis_index("fsdp")
    section_index = lax.axis_index("section")
    last_section = section_size - 1
    is_last = section_index == last_section
    section_bits = section_size.bit_length() - 1
    y_size = 1 << ((fsdp_size.bit_length() - 1) // 2)
    z_size = fsdp_size // y_size
    y_place = member % y_size
    z_place = member // y_size
    tasks, head_rows, outs = head_weight.shape

    hidden = activations[0]
    rows, features = hidden.shape
    weight = trunk_weight[0]
    fused = kernels_fit(rows, features, fsdp_size, section_size)
    if fused:
        pre, feature_all = project(hidden, norm_gain, weight, fsdp_size, section_size)
        feature_all = feature_all.reshape(fsdp_size * rows, features // fsdp_size)
    else:
        normed = (rms_scale(hidden.astype(F32)) * norm_gain[0]).astype(BF)
        feature_block = lax.all_to_all(normed, "fsdp", split_axis=1, concat_axis=0, tiled=True)
        pre = project_permuted(feature_block, weight, rows, y_size, z_size, y_place, z_place)
        feature_all = from_last(feature_block, section_index, section_size)

    wanted = head_weight[task_of[:, 0]]
    if head_rows % section_size == 0 and (head_rows // section_size) % 16 == 0:
        share = head_rows // section_size
        part = lax.dynamic_slice_in_dim(wanted, section_index * share, share, 1)
        part = lax.all_to_all(part, "fsdp", split_axis=0, concat_axis=0, tiled=True)
        part = lax.all_gather(part, "section", axis=1, tiled=True)
    else:
        part = lax.all_to_all(wanted, "fsdp", split_axis=0, concat_axis=0, tiled=True)
    head_w = part.reshape(features, outs)

    output = (hidden.astype(F32) + jax.nn.silu(pre.astype(F32))).astype(BF)
    passed = lax.ppermute(output, "section", [(i, i + 1) for i in range(section_size - 1)])

    task_id = task_of[member, 0]
    onehot = (task_of[:, 0][:, None] == jnp.arange(tasks)[None, :]).astype(F32)
    counts = rows * jnp.sum(onehot, axis=0)
    own_task = (jnp.arange(tasks) == task_id).astype(F32)
    block_loss, pullback = jax.vjp(
        lambda inner: head_loss(
            inner, head_w, head_mix[task_id], head_steps[task_id] + 1, targets, tasks
        ),
        output.astype(F32),
    )
    grad_out = pullback(jnp.ones_like(block_loss))[0]
    square = jnp.sum(grad_out * grad_out)
    pre_float = pre.astype(F32)
    sigmoid_pre = jax.nn.sigmoid(pre_float)
    slope_term = sigmoid_pre * (1.0 + pre_float * (1.0 - sigmoid_pre))
    cotangent = (grad_out * slope_term).astype(BF)

    col_width = features // section_size
    sums = jnp.concatenate([own_task * square, own_task * block_loss])
    if fused:
        stats = jnp.broadcast_to(jnp.pad(sums, (0, 128 - 2 * tasks))[None, :], (8, 128))
        column_block, table = gather(cotangent, stats, fsdp_size, section_size)
        sums = jnp.sum(table[:, :, 0, : 2 * tasks], axis=(0, 1))
        column_block = column_block.reshape(fsdp_size * rows, col_width)
        order = onehot.reshape(z_size, y_size, tasks).swapaxes(0, 1).reshape(fsdp_size, tasks)
    else:
        cols = cotangent.reshape(rows, section_size, col_width)
        for bit in reversed(range(section_bits)):
            half = cols.reshape(rows, 2, cols.shape[1] // 2, col_width)
            low, high = half[:, 0], half[:, 1]
            got = lax.ppermute(low, "section", spread_pairs(section_size, bit))
            cols = jnp.where(section_index >> bit & 1 == 0, got, high)
        column_block = lax.all_gather(cols[:, 0], "fsdp", axis=0, tiled=True)
        sums = lax.psum(jnp.where(is_last, sums, jnp.zeros_like(sums)), ("section", "fsdp"))
        order = onehot
    norm_sums, loss_sums = sums[:tasks], sums[tasks:]
    grad_norms = jnp.sqrt(norm_sums)
    ratios = jnp.mean(grad_norms) * loss_ratio**ALPHA / grad_norms
    task_weights = tasks * ratios / jnp.sum(ratios)
    task_losses = loss_sums / (counts * outs)

    block_weight = jnp.sum(order * task_weights[None, :], axis=1)
    scaled = (
        column_block.reshape(fsdp_size, rows, col_width).astype(F32)
        * block_weight[:, None, None]
    ).astype(BF)
    joined_grad = lax.dot_general(
        feature_all,
        scaled.reshape(fsdp_size * rows, col_width),
        (((0,), (0,)), ((), ())),
        preferred_element_type=F32,
    )
    return (passed[None], joined_grad, task_weights, task_losses)


def solution(mesh):
    return jax.shard_map(
        local,
        mesh=mesh,
        in_specs=(
            P("section", "fsdp", None),
            P("section", None),
            P("section", "fsdp", None),
            P(None, "fsdp", None),
            P(),
            P(),
            P(),
            P(),
            P("fsdp", None),
        ),
        out_specs=(P("section", "fsdp", None), P("fsdp", "section"), P(), P()),
        check_vma=False,
    )
```

```python
import functools

import jax
import jax.numpy as jnp
from jax import lax
from jax.experimental import pallas as pl
from jax.experimental.pallas import tpu as pltpu
from jax.sharding import PartitionSpec as P

EPS = 1e-05
ALPHA = 1.5
BF = jnp.bfloat16
F32 = jnp.float32
MESH = pl.DeviceIdType.MESH
CHUNKS = 8
HALVES = 2
VMEM_MAX = 48 << 20


def rms_scale(values):
    return values * lax.rsqrt(jnp.mean(values * values, axis=-1, keepdims=True) + EPS)


def head_loss(blocks, head_w, mix_w, step_total, target, tasks):
    head_in = rms_scale(blocks).astype(BF)
    outputs = jnp.dot(head_in, head_w, preferred_element_type=F32)
    for depth_index in range(tasks):
        active = (depth_index < step_total).astype(F32)
        outputs = outputs + active * jnp.tanh(
            jnp.dot(outputs, mix_w, precision=lax.Precision.HIGHEST)
        )
    error_term = outputs - target.astype(F32)
    return 0.5 * jnp.sum(error_term * error_term)


def line_reduce_scatter(blocks, place, count, inner, stride):
    if count == 1:
        return blocks[0].astype(F32)
    devices = lax.axis_size("fsdp")

    def pairs(step, limit):
        found = []
        for index in range(devices):
            spot = index // stride % count
            if 0 <= spot + step < count and limit(spot):
                found.append((index, index + step * stride))
        return found

    def pick(position):
        return lax.dynamic_index_in_dim(blocks, jnp.clip(position, 0, count - 1), 0, keepdims=False)

    own = pick(place).astype(F32)
    if count == 2:
        swap = pairs(1, lambda s: True) + pairs(-1, lambda s: True)
        return own + lax.ppermute(pick(1 - place).astype(BF), "fsdp", swap).astype(F32)
    right = left = None
    for t in range(1, count):
        send_right = pick(count - t + place)
        send_left = pick(place - count + t)
        if right is not None:
            send_right = send_right.astype(F32) + right.astype(F32)
            send_left = send_left.astype(F32) + left.astype(F32)
        right = lax.ppermute(send_right.astype(BF), "fsdp", pairs(1, lambda s: s <= t - 1))
        left = lax.ppermute(send_left.astype(BF), "fsdp", pairs(-1, lambda s: s >= count - t))
    return own + right.astype(F32) + left.astype(F32)


def spread_pairs(size, bit):
    low = (1 << (bit + 1)) - 1
    return [(i, i ^ (1 << bit)) for i in range(size) if i & low == low]


def remote(src, dst, send, recv, **place):
    return pltpu.make_async_remote_copy(
        src_ref=src, dst_ref=dst, send_sem=send, recv_sem=recv, device_id=place,
        device_id_type=MESH,
    )


def greet(fsdp, sections):
    me, section = lax.axis_index("fsdp"), lax.axis_index("section")
    barrier = pltpu.get_barrier_semaphore()
    for j in range(1, fsdp):
        pl.semaphore_signal(
            barrier, inc=1, device_id={"fsdp": lax.rem(me + j, fsdp)}, device_id_type=MESH
        )
    for j in range(1, sections):
        pl.semaphore_signal(
            barrier, inc=1, device_id={"section": lax.rem(section + j, sections)},
            device_id_type=MESH,
        )
    pl.semaphore_wait(barrier, fsdp + sections - 2)


def project_kernel(
    fsdp, sections, planes, chunks,
    hidden, gain, weight, wanted, pre, feat, head,
    normed, tokens, part, y_in, z_in, z_in0, head_in,
    tok_send, tok_recv, y_send, y_recv, z_send, z_recv, f_send, f_recv,
    h_send, h_recv, hx_send, hx_recv, go,
):
    me, section = lax.axis_index("fsdp"), lax.axis_index("section")
    y, z = lax.rem(me, 2), me // 2
    rows, features = hidden.shape
    depth = features // fsdp
    width = features // chunks
    last = sections - 1
    greet(fsdp, sections)

    @pl.loop(0, rows // 16)
    def _(i):
        r = pl.ds(pl.multiple_of(i * 16, 16), 16)
        normed[r, :] = (rms_scale(hidden[r, :].astype(F32)) * gain[...]).astype(BF)

    def token_copy(lane, j):
        to = lax.rem(z + j, planes) * 2 + (1 - y if lane == 0 else y)
        return remote(
            normed.at[:, pl.ds(pl.multiple_of(to * depth, 128), depth)], tokens.at[y, z],
            tok_send.at[lane, j], tok_recv.at[lane, j], fsdp=to,
        )

    share = head_in.shape[1]

    def head_copy(j):
        to = lax.rem(me + j, fsdp)
        return remote(
            wanted.at[to, pl.ds(pl.multiple_of(section * share, 16), share)], head_in.at[me],
            h_send.at[j - 1], h_recv.at[j - 1], fsdp=to,
        )

    def head_forward(source):
        return remote(
            head_in, head.at[:, source], hx_send, hx_recv.at[source], section=last
        )

    for j in range(planes):
        token_copy(0, j).start()
    tokens[y, z] = normed[:, pl.ds(pl.multiple_of(me * depth, 128), depth)]
    head_in[me] = wanted[me, pl.ds(pl.multiple_of(section * share, 16), share)]
    for j in range(planes):
        token_copy(0, j).wait_send()
    for j in range(1, planes):
        token_copy(1, j).start()
    for j in range(1, fsdp):
        head_copy(j).start()
    for j in range(planes):
        token_copy(0, j).wait_recv()

    def feature_copy(to):
        return remote(tokens, feat, f_send.at[to], f_recv, section=to)

    def y_copy(c):
        return remote(
            part.at[c, 1 - y], y_in.at[c], y_send.at[c], y_recv.at[c], fsdp=z * 2 + 1 - y
        )

    def y_copy0():
        return remote(
            part.at[0, 1 - y, z], y_in.at[0, 0], y_send.at[0], y_recv.at[0], fsdp=z * 2 + 1 - y
        )

    def z_copy(c, way, t):
        d = planes - t + z if way == 0 else z - planes + t
        d = jnp.minimum(jnp.maximum(d, 0), planes - 1)
        to = jnp.minimum(z + 1, planes - 1) if way == 0 else jnp.maximum(z - 1, 0)
        if isinstance(c, int):
            src, dst = part.at[0, :, d], z_in0.at[way, t - 1]
        else:
            src, dst = part.at[c, y, d], z_in.at[c, way, t - 1]
        return d, remote(
            src, dst, z_send.at[c, way, t - 1], z_recv.at[c, way, t - 1], fsdp=to * 2 + y
        )

    def sends(way, t):
        if way == 0:
            return (z <= t - 1) & (z < planes - 1)
        return (z >= planes - t) & (z > 0)

    def receives(way, t):
        if way == 0:
            return (z >= 1) & (z <= t)
        return (z <= planes - 2) & (z >= planes - 1 - t)

    def z_start(c, t):
        for way in range(2):
            d, copy = z_copy(c, way, t)
            if t > 1:

                @pl.when(sends(way, t) & receives(way, t - 1))
                def _():
                    z_copy(c, way, t - 1)[1].wait_recv()
                    if isinstance(c, int):
                        for k in range(2):
                            part[0, k, d] = (
                                part[0, k, d].astype(F32) + z_in0[way, t - 2, k].astype(F32)
                            ).astype(BF)
                    else:
                        part[c, y, d] = (
                            part[c, y, d].astype(F32) + z_in[c, way, t - 2].astype(F32)
                        ).astype(BF)

            @pl.when(sends(way, t))
            def _():
                copy.start()

    def z_last(c):
        t = planes - 1
        for way in range(2):

            @pl.when(receives(way, t))
            def _():
                z_copy(c, way, t)[1].wait_recv()
                if isinstance(c, int):
                    for k in range(2):
                        part[0, k, z] = (
                            part[0, k, z].astype(F32) + z_in0[way, t - 1, k].astype(F32)
                        ).astype(BF)
                else:
                    part[c, y, z] = (
                        part[c, y, z].astype(F32) + z_in[c, way, t - 1].astype(F32)
                    ).astype(BF)

    ahead = min(3, chunks - 1)

    def multiply(c, lane):
        block = weight[:, pl.ds(pl.multiple_of(c * width, 128), width)]
        part[c, lane] = (
            jnp.dot(tokens[lane].reshape(planes * rows, depth), block, preferred_element_type=F32)
            .astype(BF)
            .reshape(planes, rows, width)
        )

    beside = last - 1

    @pl.loop(1, chunks + 1)
    def _(i):
        c = lax.rem(i, chunks)
        multiply(c, 1 - y)

        @pl.when((i <= ahead) & (section != beside))
        def _():
            y_copy(i).start()

    for j in range(1, planes):
        token_copy(1, j).wait_recv()

    @pl.when(section == last)
    def _():
        for to in range(last):
            feature_copy(to).start()
        feat[...] = tokens[...]

    @pl.loop(0, chunks)
    def _(c):
        multiply(c, y)

        @pl.when((c == 0) & (section != beside))
        def _():
            z_start(0, 1)

    for j in range(1, fsdp):
        head_copy(j).wait_recv()

    @pl.when(section != last)
    def _():
        head_forward(section).start()

    @pl.when(section == last)
    def _():
        for f in range(fsdp):
            head[f, last] = head_in[f]

    @pl.when(section == beside)
    def _():
        pl.semaphore_wait(go, 1)
        for i in range(1, ahead + 1):
            y_copy(i).start()
        z_start(0, 1)

    @pl.loop(1, chunks + planes - 1)
    def _(i):
        for t in range(1, planes):

            @pl.when(i == t)
            def _():
                if t < planes - 1:
                    z_start(0, t + 1)
                else:
                    z_last(0)
                    y_copy0().start()

        @pl.when(i < chunks)
        def _():
            y_copy(i).wait_recv()

            @pl.when(i + ahead < chunks)
            def _():
                y_copy(i + ahead).start()

            @pl.when((i == chunks - 2) & (section == last))
            def _():
                pl.semaphore_signal(
                    go, inc=1, device_id={"section": beside}, device_id_type=MESH
                )

            for d in range(planes):
                part[i, y, d] = (part[i, y, d].astype(F32) + y_in[i, d].astype(F32)).astype(BF)
            z_start(i, 1)

        for t in range(1, planes - 1):
            c = i - t

            @pl.when((c >= 1) & (c < chunks))
            def _():
                z_start(c, t + 1)

        c = i - (planes - 1)

        @pl.when((c >= 1) & (c < chunks))
        def _():
            z_last(c)
            pre[:, pl.ds(pl.multiple_of(c * width, 128), width)] = part[c, y, z]

    y_copy0().wait_recv()
    pre[:, pl.ds(0, width)] = (part[0, y, z].astype(F32) + y_in[0, 0].astype(F32)).astype(BF)

    @pl.when(section != last)
    def _():
        feature_copy(0).wait_recv()

    @pl.when(section == last)
    def _():
        for to in range(last):
            feature_copy(to).wait_send()

    @pl.when(section != last)
    def _():
        head[...] = jnp.zeros_like(head)
        head_forward(section).wait_send()

    @pl.when(section == last)
    def _():
        for source in range(last):
            head_forward(source).wait_recv()

    for j in range(1, planes):
        token_copy(1, j).wait_send()
    for j in range(1, fsdp):
        head_copy(j).wait_send()
    y_copy0().wait_send()
    for t in range(1, planes):
        for way in range(2):

            @pl.when(sends(way, t))
            def _():
                z_copy(0, way, t)[1].wait_send()

    @pl.loop(1, chunks)
    def _(c):
        y_copy(c).wait_send()
        for t in range(1, planes):
            for way in range(2):

                @pl.when(sends(way, t))
                def _():
                    z_copy(c, way, t)[1].wait_send()


def project(hidden, gain, weight, wanted, fsdp, sections):
    rows, features = hidden.shape
    share, outs = wanted.shape[1] // sections, wanted.shape[2]
    planes, chunks = fsdp // 2, CHUNKS
    depth, width = features // fsdp, features // chunks
    dma = pltpu.SemaphoreType.DMA
    vmem = pl.BlockSpec(memory_space=pltpu.VMEM)
    return pl.pallas_call(
        functools.partial(project_kernel, fsdp, sections, planes, chunks),
        out_shape=(
            jax.ShapeDtypeStruct((rows, features), BF),
            jax.ShapeDtypeStruct((2, planes, rows, depth), BF),
            jax.ShapeDtypeStruct((fsdp, sections, share, outs), BF),
        ),
        in_specs=[vmem] * 4,
        out_specs=(vmem, vmem, vmem),
        scratch_shapes=[
            pltpu.VMEM((rows, features), BF),
            pltpu.VMEM((2, planes, rows, depth), BF),
            pltpu.VMEM((chunks, 2, planes, rows, width), BF),
            pltpu.VMEM((chunks, planes, rows, width), BF),
            pltpu.VMEM((chunks, 2, planes - 1, rows, width), BF),
            pltpu.VMEM((2, planes - 1, 2, rows, width), BF),
            pltpu.VMEM((fsdp, share, outs), BF),
            dma((2, planes)),
            dma((2, planes)),
            dma((chunks,)),
            dma((chunks,)),
            dma((chunks, 2, planes - 1)),
            dma((chunks, 2, planes - 1)),
            dma((sections,)),
            dma,
            dma((fsdp - 1,)),
            dma((fsdp - 1,)),
            dma,
            dma((sections,)),
            pltpu.SemaphoreType.REGULAR,
        ],
        compiler_params=pltpu.CompilerParams(
            collective_id=0, has_side_effects=True, vmem_limit_bytes=VMEM_MAX
        ),
        cost_estimate=pl.CostEstimate(
            flops=2 * fsdp * rows * depth * features, bytes_accessed=1 << 23, transcendentals=0
        ),
    )(hidden, gain, weight, wanted)


def gather_kernel(
    fsdp, sections, planes,
    tasks, cot, stats, feat, order, powers, joined, sums, weights, cols, table,
    x_send, x_recv, sx_send, sx_recv, st_send, st_recv, z_send, z_recv, y_send, y_recv,
):
    me, section = lax.axis_index("fsdp"), lax.axis_index("section")
    y, z = lax.rem(me, 2), me // 2
    last = sections - 1
    rows, features = cot.shape
    width = features // sections
    size = rows // HALVES
    greet(fsdp, sections)

    def stats_x(to):
        return remote(stats, table.at[y, z], sx_send.at[to], sx_recv, section=to)

    def cols_x(to, h):
        return remote(
            cot.at[pl.ds(h * size, size), pl.ds(to * width, width)], cols.at[y, z, h],
            x_send.at[to, h], x_recv.at[h], section=to,
        )

    def stats_f(j):
        return remote(
            table.at[y, z], table.at[y, z], st_send.at[j - 1], st_recv.at[j - 1],
            fsdp=lax.rem(me + j, fsdp),
        )

    def y_copy(plane, h):
        block = cols.at[y, plane, h]
        return remote(
            block, block, y_send.at[plane, h], y_recv.at[plane, h], fsdp=z * 2 + 1 - y
        )

    def z_copy(way, t, h):
        if way == 0:
            plane, to = jnp.maximum(z - t + 1, 0), jnp.minimum(z + 1, planes - 1)
        else:
            plane, to = jnp.minimum(z + t - 1, planes - 1), jnp.maximum(z - 1, 0)
        block = cols.at[y, plane, h]
        return remote(
            block, block, z_send.at[way, t - 1, h], z_recv.at[way, t - 1, h], fsdp=to * 2 + y
        )

    def sends(way, t):
        if way == 0:
            return (z < planes - 1) & (z - t + 1 >= 0)
        return (z > 0) & (z + t - 1 <= planes - 1)

    def receives(way, t):
        return z - t >= 0 if way == 0 else z + t <= planes - 1

    @pl.when(section == last)
    def _():
        for to in range(last):
            stats_x(to).start()
        for h in range(HALVES):
            for to in range(last):
                cols_x(to, h).start()
        table[y, z] = stats[...]
        for h in range(HALVES):
            cols[y, z, h] = cot[pl.ds(h * size, size), pl.ds(last * width, width)]

    @pl.when(section != last)
    def _():
        stats_x(0).wait_recv()

    for j in range(1, fsdp):
        stats_f(j).start()

    def add(lane, plane):
        block = cols[lane, plane].reshape(rows, width).astype(F32)
        row = order[pl.ds(lane * planes + plane, 1)][0]
        scale = jnp.sum(row * weights[...], axis=1, keepdims=True)[:1]
        block = (block * scale).astype(BF)
        joined[...] += lax.dot_general(
            feat[lane, plane], block, (((0,), (0,)), ((), ())), preferred_element_type=F32
        )

    def add_across(plane):
        for h in range(HALVES):
            y_copy(plane, h).wait_recv()
        add(1 - y, plane)

    joined[...] = jnp.zeros_like(joined)
    for h in range(HALVES):

        @pl.when(section != last)
        def _():
            cols_x(0, h).wait_recv()

        for way in range(2):

            @pl.when(sends(way, 1))
            def _():
                z_copy(way, 1, h).start()

        y_copy(z, h).start()
    for j in range(1, fsdp):
        stats_f(j).wait()
    total = jnp.sum(table[...], axis=(0, 1))
    sums[...] = total
    lane_number = lax.broadcasted_iota(jnp.int32, total.shape, 1)
    counted = lane_number < tasks
    norms = jnp.sqrt(total)
    mean_norm = jnp.sum(jnp.where(counted, norms, 0.0), axis=1, keepdims=True) / tasks
    ratios = jnp.where(counted, mean_norm * powers[...] / norms, 0.0)
    weights[...] = tasks * ratios / jnp.sum(ratios, axis=1, keepdims=True)

    for t in range(1, planes):
        for h in range(HALVES):
            for way in range(2):

                @pl.when(receives(way, t))
                def _():
                    z_copy(way, t, h).wait_recv()
                    y_copy(z - t if way == 0 else z + t, h).start()

                if t < planes - 1:

                    @pl.when(sends(way, t + 1))
                    def _():
                        z_copy(way, t + 1, h).start()

        if t == 1:
            add(y, z)
            add_across(z)
        for way in range(2):

            @pl.when(receives(way, t))
            def _():
                add(y, z - t if way == 0 else z + t)

            if t > 1:

                @pl.when(receives(way, t - 1))
                def _():
                    add_across(z - t + 1 if way == 0 else z + t - 1)

    for way in range(2):

        @pl.when(receives(way, planes - 1))
        def _():
            add_across(z - planes + 1 if way == 0 else z + planes - 1)

    for plane in range(planes):
        for h in range(HALVES):
            y_copy(plane, h).wait_send()
    for t in range(1, planes):
        for h in range(HALVES):
            for way in range(2):

                @pl.when(sends(way, t))
                def _():
                    z_copy(way, t, h).wait_send()

    @pl.when(section == last)
    def _():
        for to in range(last):
            stats_x(to).wait_send()
            for h in range(HALVES):
                cols_x(to, h).wait_send()


def joined_product(cot, stats, feat, order, powers, tasks, fsdp, sections):
    rows, features = cot.shape
    planes = fsdp // 2
    width = features // sections
    dma = pltpu.SemaphoreType.DMA
    vmem = pl.BlockSpec(memory_space=pltpu.VMEM)
    return pl.pallas_call(
        functools.partial(gather_kernel, fsdp, sections, planes, tasks),
        out_shape=(
            jax.ShapeDtypeStruct((feat.shape[3], width), F32),
            jax.ShapeDtypeStruct(stats.shape, F32),
            jax.ShapeDtypeStruct(stats.shape, F32),
        ),
        in_specs=[vmem] * 5,
        out_specs=(vmem, vmem, vmem),
        scratch_shapes=[
            pltpu.VMEM((2, planes, HALVES, rows // HALVES, width), BF),
            pltpu.VMEM((2, planes) + stats.shape, F32),
            dma((sections, HALVES)),
            dma((HALVES,)),
            dma((sections,)),
            dma,
            dma((fsdp - 1,)),
            dma((fsdp - 1,)),
            dma((2, planes - 1, HALVES)),
            dma((2, planes - 1, HALVES)),
            dma((planes, HALVES)),
            dma((planes, HALVES)),
        ],
        compiler_params=pltpu.CompilerParams(
            collective_id=1, has_side_effects=True, vmem_limit_bytes=VMEM_MAX
        ),
        cost_estimate=pl.CostEstimate(flops=0, bytes_accessed=1 << 23, transcendentals=0),
    )(cot, stats, feat, order, powers)


def kernels_fit(rows, features, fsdp, sections, head_rows, tasks):
    if fsdp < 4 or fsdp % 2 or sections < 2:
        return False
    planes = fsdp // 2
    block = rows * features * 2
    planned = block * (2 * planes + planes + 2 * planes - 2 + 10) + features // fsdp * features * 2
    return (
        planned <= VMEM_MAX * 3 // 4
        and rows % (16 * HALVES) == 0
        and CHUNKS >= planes + 1
        and features % (128 * CHUNKS) == 0
        and features % (128 * fsdp) == 0
        and features % (128 * sections) == 0
        and head_rows % (16 * sections) == 0
        and 2 * tasks <= 128
        and 1 << ((fsdp.bit_length() - 1) // 2) == 2
    )


def project_permuted(feature_block, weight, rows, y_size, z_size, y_place, z_place):
    features = weight.shape[1]
    chunks = 4
    width = features // chunks
    pieces = []
    for c in range(chunks):
        partial = jnp.dot(
            feature_block, weight[:, c * width : (c + 1) * width], preferred_element_type=F32
        ).astype(BF)
        partial = partial.reshape(z_size, y_size, rows, width)
        if c == 1:
            partial = line_reduce_scatter(partial, z_place, z_size, y_size, y_size)
            total = line_reduce_scatter(partial, y_place, y_size, 1, 1)
        else:
            partial = line_reduce_scatter(partial.swapaxes(0, 1), y_place, y_size, 1, 1)
            total = line_reduce_scatter(partial, z_place, z_size, y_size, y_size)
        pieces.append(total.astype(BF))
    return jnp.concatenate(pieces, axis=1)


def from_last(feature_all, section_index, section_size):
    for bit in reversed(range(section_size.bit_length() - 1)):
        got = lax.ppermute(feature_all, "section", spread_pairs(section_size, bit))
        takes = (section_index >> bit & 1 == 0) & (
            section_index & ((1 << bit) - 1) == (1 << bit) - 1
        )
        feature_all = jnp.where(takes, got, feature_all)
    return feature_all


def local(
    activations,
    norm_gain,
    trunk_weight,
    head_weight,
    head_mix,
    head_steps,
    task_of,
    loss_ratio,
    targets,
):
    fsdp_size = lax.axis_size("fsdp")
    section_size = lax.axis_size("section")
    member = lax.axis_index("fsdp")
    section_index = lax.axis_index("section")
    last_section = section_size - 1
    is_last = section_index == last_section
    section_bits = section_size.bit_length() - 1
    y_size = 1 << ((fsdp_size.bit_length() - 1) // 2)
    z_size = fsdp_size // y_size
    y_place = member % y_size
    z_place = member // y_size
    tasks, head_rows, outs = head_weight.shape

    hidden = activations[0]
    rows, features = hidden.shape
    weight = trunk_weight[0]
    fused = kernels_fit(rows, features, fsdp_size, section_size, head_rows, tasks)
    wanted = head_weight[task_of[:, 0]]
    if fused:
        pre, feature_all, head_w = project(
            hidden, norm_gain, weight, wanted, fsdp_size, section_size
        )
    else:
        normed = (rms_scale(hidden.astype(F32)) * norm_gain[0]).astype(BF)
        feature_block = lax.all_to_all(normed, "fsdp", split_axis=1, concat_axis=0, tiled=True)
        pre = project_permuted(feature_block, weight, rows, y_size, z_size, y_place, z_place)
        feature_all = from_last(feature_block, section_index, section_size)
        part = wanted
        if head_rows % (16 * section_size) == 0:
            share = head_rows // section_size
            part = lax.dynamic_slice_in_dim(part, section_index * share, share, 1)
        part = lax.all_to_all(part, "fsdp", split_axis=0, concat_axis=0, tiled=True)
        if part.shape[1] != head_rows:
            part = lax.all_gather(part, "section", axis=1, tiled=True)
        head_w = part
    head_w = head_w.reshape(features, outs)

    output = (hidden.astype(F32) + jax.nn.silu(pre.astype(F32))).astype(BF)
    passed = lax.ppermute(output, "section", [(i, i + 1) for i in range(section_size - 1)])

    task_id = task_of[member, 0]
    onehot = (task_of[:, 0][:, None] == jnp.arange(tasks)[None, :]).astype(F32)
    counts = rows * jnp.sum(onehot, axis=0)
    own_task = (jnp.arange(tasks) == task_id).astype(F32)

    def head_pass(output, pre, head_w):
        block_loss, pullback = jax.vjp(
            lambda inner: head_loss(
                inner, head_w, head_mix[task_id], head_steps[task_id] + 1, targets, tasks
            ),
            output.astype(F32),
        )
        grad_out = pullback(jnp.ones_like(block_loss))[0]
        square = jnp.sum(grad_out * grad_out)
        pre_float = pre.astype(F32)
        sigmoid_pre = jax.nn.sigmoid(pre_float)
        slope_term = sigmoid_pre * (1.0 + pre_float * (1.0 - sigmoid_pre))
        cotangent = (grad_out * slope_term).astype(BF)
        return cotangent, jnp.concatenate([own_task * square, own_task * block_loss])

    if fused:
        cotangent, sums = lax.cond(
            is_last,
            head_pass,
            lambda output, pre, head_w: (jnp.zeros_like(output), jnp.zeros((2 * tasks,), F32)),
            output, pre, head_w,
        )
    else:
        cotangent, sums = head_pass(output, pre, head_w)
    col_width = features // section_size
    if fused:
        order = onehot.reshape(z_size, y_size, tasks).swapaxes(0, 1).reshape(fsdp_size, tasks)
        order = jnp.pad(order, ((0, 0), (0, 128 - tasks)))
        order = jnp.broadcast_to(order[:, None, :], (fsdp_size, 8, 128))
        powers = jnp.pad(loss_ratio**ALPHA, (0, 128 - tasks), constant_values=1.0)
        joined_grad, sums, weights = joined_product(
            cotangent,
            jnp.broadcast_to(jnp.pad(sums, (0, 128 - 2 * tasks))[None, :], (8, 128)),
            feature_all,
            order,
            jnp.broadcast_to(powers[None, :], (8, 128)),
            tasks,
            fsdp_size,
            section_size,
        )
        task_losses = sums[0, tasks : 2 * tasks] / (counts * outs)
        return (passed[None], joined_grad, weights[0, :tasks], task_losses)
    cols = cotangent.reshape(rows, section_size, col_width)
    for bit in reversed(range(section_bits)):
        half = cols.reshape(rows, 2, cols.shape[1] // 2, col_width)
        low, high = half[:, 0], half[:, 1]
        got = lax.ppermute(low, "section", spread_pairs(section_size, bit))
        cols = jnp.where(section_index >> bit & 1 == 0, got, high)
    column_block = lax.all_gather(cols[:, 0], "fsdp", axis=0, tiled=True)
    sums = lax.psum(jnp.where(is_last, sums, jnp.zeros_like(sums)), ("section", "fsdp"))
    norm_sums, loss_sums = sums[:tasks], sums[tasks:]
    grad_norms = jnp.sqrt(norm_sums)
    ratios = jnp.mean(grad_norms) * loss_ratio**ALPHA / grad_norms
    task_weights = tasks * ratios / jnp.sum(ratios)
    task_losses = loss_sums / (counts * outs)

    block_weight = jnp.sum(onehot * task_weights[None, :], axis=1)
    scaled = (
        column_block.reshape(fsdp_size, rows, col_width).astype(F32)
        * block_weight[:, None, None]
    ).astype(BF)
    joined_grad = lax.dot_general(
        feature_all,
        scaled.reshape(fsdp_size * rows, col_width),
        (((0,), (0,)), ((), ())),
        preferred_element_type=F32,
    )
    return (passed[None], joined_grad, task_weights, task_losses)


def solution(mesh):
    return jax.shard_map(
        local,
        mesh=mesh,
        in_specs=(
            P("section", "fsdp", None),
            P("section", None),
            P("section", "fsdp", None),
            P(None, "fsdp", None),
            P(),
            P(),
            P(),
            P(),
            P("fsdp", None),
        ),
        out_specs=(P("section", "fsdp", None), P("fsdp", "section"), P(), P()),
        check_vma=False,
    )
```

```python
import functools

import jax
import jax.numpy as jnp
from jax import lax
from jax.experimental import pallas as pl
from jax.experimental.pallas import tpu as pltpu
from jax.sharding import PartitionSpec as P

EPS = 1e-05
ALPHA = 1.5
BF = jnp.bfloat16
F32 = jnp.float32
MESH = pl.DeviceIdType.MESH
CHUNKS = 8
HALVES = 2
VMEM_MAX = 48 << 20


def rms_scale(values):
    return values * lax.rsqrt(jnp.mean(values * values, axis=-1, keepdims=True) + EPS)


def head_loss(blocks, head_w, mix_w, step_total, target, tasks):
    head_in = rms_scale(blocks).astype(BF)
    outputs = jnp.dot(head_in, head_w, preferred_element_type=F32)
    for depth_index in range(tasks):
        active = (depth_index < step_total).astype(F32)
        outputs = outputs + active * jnp.tanh(
            jnp.dot(outputs, mix_w, precision=lax.Precision.HIGHEST)
        )
    error_term = outputs - target.astype(F32)
    return 0.5 * jnp.sum(error_term * error_term)


def line_reduce_scatter(blocks, place, count, inner, stride):
    if count == 1:
        return blocks[0].astype(F32)
    devices = lax.axis_size("fsdp")

    def pairs(step, limit):
        found = []
        for index in range(devices):
            spot = index // stride % count
            if 0 <= spot + step < count and limit(spot):
                found.append((index, index + step * stride))
        return found

    def pick(position):
        return lax.dynamic_index_in_dim(blocks, jnp.clip(position, 0, count - 1), 0, keepdims=False)

    own = pick(place).astype(F32)
    if count == 2:
        swap = pairs(1, lambda s: True) + pairs(-1, lambda s: True)
        return own + lax.ppermute(pick(1 - place).astype(BF), "fsdp", swap).astype(F32)
    right = left = None
    for t in range(1, count):
        send_right = pick(count - t + place)
        send_left = pick(place - count + t)
        if right is not None:
            send_right = send_right.astype(F32) + right.astype(F32)
            send_left = send_left.astype(F32) + left.astype(F32)
        right = lax.ppermute(send_right.astype(BF), "fsdp", pairs(1, lambda s: s <= t - 1))
        left = lax.ppermute(send_left.astype(BF), "fsdp", pairs(-1, lambda s: s >= count - t))
    return own + right.astype(F32) + left.astype(F32)


def spread_pairs(size, bit):
    low = (1 << (bit + 1)) - 1
    return [(i, i ^ (1 << bit)) for i in range(size) if i & low == low]


def remote(src, dst, send, recv, **place):
    return pltpu.make_async_remote_copy(
        src_ref=src, dst_ref=dst, send_sem=send, recv_sem=recv, device_id=place,
        device_id_type=MESH,
    )


def greet(fsdp, sections):
    me, section = lax.axis_index("fsdp"), lax.axis_index("section")
    barrier = pltpu.get_barrier_semaphore()
    for j in range(1, fsdp):
        pl.semaphore_signal(
            barrier, inc=1, device_id={"fsdp": lax.rem(me + j, fsdp)}, device_id_type=MESH
        )
    for j in range(1, sections):
        pl.semaphore_signal(
            barrier, inc=1, device_id={"section": lax.rem(section + j, sections)},
            device_id_type=MESH,
        )
    pl.semaphore_wait(barrier, fsdp + sections - 2)


def project_kernel(
    fsdp, sections, planes, chunks,
    hidden, gain, weight, wanted, pre, out, feat, head,
    normed, tokens, part, y_in, z_in, z_in0, head_in,
    tok_send, tok_recv, y_send, y_recv, z_send, z_recv, f_send, f_recv,
    h_send, h_recv, hx_send, hx_recv, go,
):
    me, section = lax.axis_index("fsdp"), lax.axis_index("section")
    y, z = lax.rem(me, 2), me // 2
    rows, features = hidden.shape
    depth = features // fsdp
    width = features // chunks
    last = sections - 1
    greet(fsdp, sections)

    @pl.loop(0, rows // 16)
    def _(i):
        r = pl.ds(pl.multiple_of(i * 16, 16), 16)
        normed[r, :] = (rms_scale(hidden[r, :].astype(F32)) * gain[...]).astype(BF)

    def token_copy(lane, j):
        to = lax.rem(z + j, planes) * 2 + (1 - y if lane == 0 else y)
        return remote(
            normed.at[:, pl.ds(pl.multiple_of(to * depth, 128), depth)], tokens.at[y, z],
            tok_send.at[lane, j], tok_recv.at[lane, j], fsdp=to,
        )

    share = head_in.shape[1]

    def head_copy(j):
        to = lax.rem(me + j, fsdp)
        return remote(
            wanted.at[to, pl.ds(pl.multiple_of(section * share, 16), share)], head_in.at[me],
            h_send.at[j - 1], h_recv.at[j - 1], fsdp=to,
        )

    def head_forward(source):
        return remote(
            head_in, head.at[:, source], hx_send, hx_recv.at[source], section=last
        )

    for j in range(planes):
        token_copy(0, j).start()
    tokens[y, z] = normed[:, pl.ds(pl.multiple_of(me * depth, 128), depth)]
    head_in[me] = wanted[me, pl.ds(pl.multiple_of(section * share, 16), share)]
    for j in range(planes):
        token_copy(0, j).wait_send()
    for j in range(1, planes):
        token_copy(1, j).start()
    for j in range(1, fsdp):
        head_copy(j).start()
    def feature_copy(to):
        return remote(tokens, feat, f_send.at[to], f_recv, section=to)

    def y_copy(c):
        return remote(
            part.at[c, 1 - y], y_in.at[c], y_send.at[c], y_recv.at[c], fsdp=z * 2 + 1 - y
        )

    def y_copy0():
        return remote(
            part.at[0, 1 - y, z], y_in.at[0, 0], y_send.at[0], y_recv.at[0], fsdp=z * 2 + 1 - y
        )

    def z_copy(c, way, t):
        d = planes - t + z if way == 0 else z - planes + t
        d = jnp.minimum(jnp.maximum(d, 0), planes - 1)
        to = jnp.minimum(z + 1, planes - 1) if way == 0 else jnp.maximum(z - 1, 0)
        if isinstance(c, int):
            src, dst = part.at[0, :, d], z_in0.at[way, t - 1]
        else:
            src, dst = part.at[c, y, d], z_in.at[c, way, t - 1]
        return d, remote(
            src, dst, z_send.at[c, way, t - 1], z_recv.at[c, way, t - 1], fsdp=to * 2 + y
        )

    def sends(way, t):
        if way == 0:
            return (z <= t - 1) & (z < planes - 1)
        return (z >= planes - t) & (z > 0)

    def receives(way, t):
        if way == 0:
            return (z >= 1) & (z <= t)
        return (z <= planes - 2) & (z >= planes - 1 - t)

    def z_start(c, t):
        for way in range(2):
            d, copy = z_copy(c, way, t)
            if t > 1:

                @pl.when(sends(way, t) & receives(way, t - 1))
                def _():
                    z_copy(c, way, t - 1)[1].wait_recv()
                    if isinstance(c, int):
                        for k in range(2):
                            part[0, k, d] = (
                                part[0, k, d].astype(F32) + z_in0[way, t - 2, k].astype(F32)
                            ).astype(BF)
                    else:
                        part[c, y, d] = (
                            part[c, y, d].astype(F32) + z_in[c, way, t - 2].astype(F32)
                        ).astype(BF)

            @pl.when(sends(way, t))
            def _():
                copy.start()

    def z_last(c):
        t = planes - 1
        for way in range(2):

            @pl.when(receives(way, t))
            def _():
                z_copy(c, way, t)[1].wait_recv()
                if isinstance(c, int):
                    for k in range(2):
                        part[0, k, z] = (
                            part[0, k, z].astype(F32) + z_in0[way, t - 1, k].astype(F32)
                        ).astype(BF)
                else:
                    part[c, y, z] = (
                        part[c, y, z].astype(F32) + z_in[c, way, t - 1].astype(F32)
                    ).astype(BF)

    ahead = min(3, chunks - 1)

    def multiply(c, lane):
        block = weight[:, pl.ds(pl.multiple_of(c * width, 128), width)]
        part[c, lane] = (
            jnp.dot(tokens[lane].reshape(planes * rows, depth), block, preferred_element_type=F32)
            .astype(BF)
            .reshape(planes, rows, width)
        )

    def finish(c, value):
        columns = pl.ds(pl.multiple_of(c * width, 128), width)
        pre[:, columns] = value
        wide = value.astype(F32)
        out[:, columns] = (
            hidden[:, columns].astype(F32) + wide * jax.nn.sigmoid(wide)
        ).astype(BF)

    beside = last - 1

    for j in range(planes):
        token_copy(0, j).wait_recv()
        d = lax.rem(z + planes - j, planes)

        @pl.loop(1, ahead + 1)
        def _(c):
            block = weight[:, pl.ds(pl.multiple_of(c * width, 128), width)]
            part[c, 1 - y, d] = jnp.dot(
                tokens[1 - y, d], block, preferred_element_type=F32
            ).astype(BF)

            @pl.when(section != beside)
            def _():
                remote(
                    part.at[c, 1 - y, d], y_in.at[c, d], y_send.at[c], y_recv.at[c],
                    fsdp=z * 2 + 1 - y,
                ).start()

    @pl.loop(ahead + 1, chunks + 1)
    def _(i):
        multiply(lax.rem(i, chunks), 1 - y)

    for j in range(1, planes):
        token_copy(1, j).wait_recv()

    @pl.when(section == last)
    def _():
        for to in range(last):
            feature_copy(to).start()
        feat[...] = tokens[...]

    @pl.loop(0, chunks)
    def _(c):
        multiply(c, y)

        @pl.when((c == 0) & (section != beside))
        def _():
            z_start(0, 1)

    for j in range(1, fsdp):
        head_copy(j).wait_recv()

    @pl.when(section != last)
    def _():
        head_forward(section).start()

    @pl.when(section == last)
    def _():
        for f in range(fsdp):
            head[f, last] = head_in[f]

    @pl.when(section == beside)
    def _():
        pl.semaphore_wait(go, 1)
        for i in range(1, ahead + 1):
            y_copy(i).start()
        z_start(0, 1)

    @pl.loop(1, chunks + planes - 1)
    def _(i):
        for t in range(1, planes):

            @pl.when(i == t)
            def _():
                if t < planes - 1:
                    z_start(0, t + 1)
                else:
                    z_last(0)
                    y_copy0().start()

        @pl.when(i < chunks)
        def _():
            y_copy(i).wait_recv()

            @pl.when(i + ahead < chunks)
            def _():
                y_copy(i + ahead).start()

            @pl.when((i == chunks - 2) & (section == last))
            def _():
                pl.semaphore_signal(
                    go, inc=1, device_id={"section": beside}, device_id_type=MESH
                )

            for d in range(planes):
                part[i, y, d] = (part[i, y, d].astype(F32) + y_in[i, d].astype(F32)).astype(BF)
            z_start(i, 1)

        for t in range(1, planes - 1):
            c = i - t

            @pl.when((c >= 1) & (c < chunks))
            def _():
                z_start(c, t + 1)

        c = i - (planes - 1)

        @pl.when((c >= 1) & (c < chunks))
        def _():
            z_last(c)
            finish(c, part[c, y, z])

    y_copy0().wait_recv()
    finish(0, (part[0, y, z].astype(F32) + y_in[0, 0].astype(F32)).astype(BF))

    @pl.when(section != last)
    def _():
        feature_copy(0).wait_recv()

    @pl.when(section == last)
    def _():
        for to in range(last):
            feature_copy(to).wait_send()

    @pl.when(section != last)
    def _():
        head[...] = jnp.zeros_like(head)
        head_forward(section).wait_send()

    @pl.when(section == last)
    def _():
        for source in range(last):
            head_forward(source).wait_recv()

    for j in range(1, planes):
        token_copy(1, j).wait_send()
    for j in range(1, fsdp):
        head_copy(j).wait_send()
    y_copy0().wait_send()
    for t in range(1, planes):
        for way in range(2):

            @pl.when(sends(way, t))
            def _():
                z_copy(0, way, t)[1].wait_send()

    @pl.loop(1, chunks)
    def _(c):
        y_copy(c).wait_send()
        for t in range(1, planes):
            for way in range(2):

                @pl.when(sends(way, t))
                def _():
                    z_copy(c, way, t)[1].wait_send()


def project(hidden, gain, weight, wanted, fsdp, sections):
    rows, features = hidden.shape
    share, outs = wanted.shape[1] // sections, wanted.shape[2]
    planes, chunks = fsdp // 2, CHUNKS
    depth, width = features // fsdp, features // chunks
    dma = pltpu.SemaphoreType.DMA
    vmem = pl.BlockSpec(memory_space=pltpu.VMEM)
    return pl.pallas_call(
        functools.partial(project_kernel, fsdp, sections, planes, chunks),
        out_shape=(
            jax.ShapeDtypeStruct((rows, features), BF),
            jax.ShapeDtypeStruct((rows, features), BF),
            jax.ShapeDtypeStruct((2, planes, rows, depth), BF),
            jax.ShapeDtypeStruct((fsdp, sections, share, outs), BF),
        ),
        in_specs=[vmem] * 4,
        out_specs=(vmem,) * 4,
        scratch_shapes=[
            pltpu.VMEM((rows, features), BF),
            pltpu.VMEM((2, planes, rows, depth), BF),
            pltpu.VMEM((chunks, 2, planes, rows, width), BF),
            pltpu.VMEM((chunks, planes, rows, width), BF),
            pltpu.VMEM((chunks, 2, planes - 1, rows, width), BF),
            pltpu.VMEM((2, planes - 1, 2, rows, width), BF),
            pltpu.VMEM((fsdp, share, outs), BF),
            dma((2, planes)),
            dma((2, planes)),
            dma((chunks,)),
            dma((chunks,)),
            dma((chunks, 2, planes - 1)),
            dma((chunks, 2, planes - 1)),
            dma((sections,)),
            dma,
            dma((fsdp - 1,)),
            dma((fsdp - 1,)),
            dma,
            dma((sections,)),
            pltpu.SemaphoreType.REGULAR,
        ],
        compiler_params=pltpu.CompilerParams(
            collective_id=0, has_side_effects=True, vmem_limit_bytes=VMEM_MAX
        ),
        cost_estimate=pl.CostEstimate(
            flops=2 * fsdp * rows * depth * features, bytes_accessed=1 << 23, transcendentals=0
        ),
    )(hidden, gain, weight, wanted)


def gather_kernel(
    fsdp, sections, planes,
    tasks, cot, stats, feat, order, powers, out, joined, sums, weights, passed, cols, table,
    x_send, x_recv, sx_send, sx_recv, st_send, st_recv, z_send, z_recv, y_send, y_recv,
    p_send, p_recv,
):
    me, section = lax.axis_index("fsdp"), lax.axis_index("section")
    y, z = lax.rem(me, 2), me // 2
    last = sections - 1
    rows, features = cot.shape
    width = features // sections
    size = rows // HALVES
    greet(fsdp, sections)

    def pass_copy():
        return remote(out, passed, p_send, p_recv, section=lax.rem(section + 1, sections))

    def stats_x(to):
        return remote(stats, table.at[y, z], sx_send.at[to], sx_recv, section=to)

    def cols_x(to, h):
        return remote(
            cot.at[pl.ds(h * size, size), pl.ds(to * width, width)], cols.at[y, z, h],
            x_send.at[to, h], x_recv.at[h], section=to,
        )

    def stats_f(j):
        return remote(
            table.at[y, z], table.at[y, z], st_send.at[j - 1], st_recv.at[j - 1],
            fsdp=lax.rem(me + j, fsdp),
        )

    def y_copy(plane, h):
        block = cols.at[y, plane, h]
        return remote(
            block, block, y_send.at[plane, h], y_recv.at[plane, h], fsdp=z * 2 + 1 - y
        )

    def z_copy(way, t, h):
        if way == 0:
            plane, to = jnp.maximum(z - t + 1, 0), jnp.minimum(z + 1, planes - 1)
        else:
            plane, to = jnp.minimum(z + t - 1, planes - 1), jnp.maximum(z - 1, 0)
        block = cols.at[y, plane, h]
        return remote(
            block, block, z_send.at[way, t - 1, h], z_recv.at[way, t - 1, h], fsdp=to * 2 + y
        )

    def sends(way, t):
        if way == 0:
            return (z < planes - 1) & (z - t + 1 >= 0)
        return (z > 0) & (z + t - 1 <= planes - 1)

    def receives(way, t):
        return z - t >= 0 if way == 0 else z + t <= planes - 1

    @pl.when(section == last)
    def _():
        for to in range(last):
            stats_x(to).start()
        for h in range(HALVES):
            for to in range(last):
                cols_x(to, h).start()
        table[y, z] = stats[...]
        for h in range(HALVES):
            cols[y, z, h] = cot[pl.ds(h * size, size), pl.ds(last * width, width)]

    @pl.when(section != last)
    def _():
        stats_x(0).wait_recv()

    for j in range(1, fsdp):
        stats_f(j).start()

    @pl.when(section != last)
    def _():
        pass_copy().start()

    @pl.when(section == 0)
    def _():
        passed[...] = jnp.zeros_like(passed)

    def add(lane, plane):
        block = cols[lane, plane].reshape(rows, width).astype(F32)
        row = order[pl.ds(lane * planes + plane, 1)][0]
        scale = jnp.sum(row * weights[...], axis=1, keepdims=True)[:1]
        block = (block * scale).astype(BF)
        joined[...] += lax.dot_general(
            feat[lane, plane], block, (((0,), (0,)), ((), ())), preferred_element_type=F32
        )

    def add_across(plane):
        for h in range(HALVES):
            y_copy(plane, h).wait_recv()
        add(1 - y, plane)

    joined[...] = jnp.zeros_like(joined)
    for h in range(HALVES):

        @pl.when(section != last)
        def _():
            cols_x(0, h).wait_recv()

        for way in range(2):

            @pl.when(sends(way, 1))
            def _():
                z_copy(way, 1, h).start()

        y_copy(z, h).start()
    for j in range(1, fsdp):
        stats_f(j).wait()
    total = jnp.sum(table[...], axis=(0, 1))
    sums[...] = total
    lane_number = lax.broadcasted_iota(jnp.int32, total.shape, 1)
    counted = lane_number < tasks
    norms = jnp.sqrt(total)
    mean_norm = jnp.sum(jnp.where(counted, norms, 0.0), axis=1, keepdims=True) / tasks
    ratios = jnp.where(counted, mean_norm * powers[...] / norms, 0.0)
    weights[...] = tasks * ratios / jnp.sum(ratios, axis=1, keepdims=True)

    for t in range(1, planes):
        for h in range(HALVES):
            for way in range(2):

                @pl.when(receives(way, t))
                def _():
                    z_copy(way, t, h).wait_recv()
                    y_copy(z - t if way == 0 else z + t, h).start()

                if t < planes - 1:

                    @pl.when(sends(way, t + 1))
                    def _():
                        z_copy(way, t + 1, h).start()

        if t == 1:
            add(y, z)
            add_across(z)
        for way in range(2):

            @pl.when(receives(way, t))
            def _():
                add(y, z - t if way == 0 else z + t)

            if t > 1:

                @pl.when(receives(way, t - 1))
                def _():
                    add_across(z - t + 1 if way == 0 else z + t - 1)

    for way in range(2):

        @pl.when(receives(way, planes - 1))
        def _():
            add_across(z - planes + 1 if way == 0 else z + planes - 1)

    @pl.when(section != 0)
    def _():
        pass_copy().wait_recv()

    @pl.when(section != last)
    def _():
        pass_copy().wait_send()

    for plane in range(planes):
        for h in range(HALVES):
            y_copy(plane, h).wait_send()
    for t in range(1, planes):
        for h in range(HALVES):
            for way in range(2):

                @pl.when(sends(way, t))
                def _():
                    z_copy(way, t, h).wait_send()

    @pl.when(section == last)
    def _():
        for to in range(last):
            stats_x(to).wait_send()
            for h in range(HALVES):
                cols_x(to, h).wait_send()


def joined_product(cot, stats, feat, order, powers, out, tasks, fsdp, sections):
    rows, features = cot.shape
    planes = fsdp // 2
    width = features // sections
    dma = pltpu.SemaphoreType.DMA
    vmem = pl.BlockSpec(memory_space=pltpu.VMEM)
    return pl.pallas_call(
        functools.partial(gather_kernel, fsdp, sections, planes, tasks),
        out_shape=(
            jax.ShapeDtypeStruct((feat.shape[3], width), F32),
            jax.ShapeDtypeStruct(stats.shape, F32),
            jax.ShapeDtypeStruct(stats.shape, F32),
            jax.ShapeDtypeStruct(out.shape, BF),
        ),
        in_specs=[vmem] * 6,
        out_specs=(vmem,) * 4,
        scratch_shapes=[
            pltpu.VMEM((2, planes, HALVES, rows // HALVES, width), BF),
            pltpu.VMEM((2, planes) + stats.shape, F32),
            dma((sections, HALVES)),
            dma((HALVES,)),
            dma((sections,)),
            dma,
            dma((fsdp - 1,)),
            dma((fsdp - 1,)),
            dma((2, planes - 1, HALVES)),
            dma((2, planes - 1, HALVES)),
            dma((planes, HALVES)),
            dma((planes, HALVES)),
            dma,
            dma,
        ],
        compiler_params=pltpu.CompilerParams(
            collective_id=1, has_side_effects=True, vmem_limit_bytes=VMEM_MAX
        ),
        cost_estimate=pl.CostEstimate(flops=0, bytes_accessed=1 << 23, transcendentals=0),
    )(cot, stats, feat, order, powers, out)


def kernels_fit(rows, features, fsdp, sections, head_rows, tasks):
    if fsdp < 4 or fsdp % 2 or sections < 2:
        return False
    planes = fsdp // 2
    block = rows * features * 2
    planned = block * (2 * planes + planes + 2 * planes - 2 + 10) + features // fsdp * features * 2
    return (
        planned <= VMEM_MAX * 3 // 4
        and rows % (16 * HALVES) == 0
        and CHUNKS >= planes + 1
        and features % (128 * CHUNKS) == 0
        and features % (128 * fsdp) == 0
        and features % (128 * sections) == 0
        and head_rows % (16 * sections) == 0
        and 2 * tasks <= 128
        and 1 << ((fsdp.bit_length() - 1) // 2) == 2
    )


def project_permuted(feature_block, weight, rows, y_size, z_size, y_place, z_place):
    features = weight.shape[1]
    chunks = 4
    width = features // chunks
    pieces = []
    for c in range(chunks):
        partial = jnp.dot(
            feature_block, weight[:, c * width : (c + 1) * width], preferred_element_type=F32
        ).astype(BF)
        partial = partial.reshape(z_size, y_size, rows, width)
        if c == 1:
            partial = line_reduce_scatter(partial, z_place, z_size, y_size, y_size)
            total = line_reduce_scatter(partial, y_place, y_size, 1, 1)
        else:
            partial = line_reduce_scatter(partial.swapaxes(0, 1), y_place, y_size, 1, 1)
            total = line_reduce_scatter(partial, z_place, z_size, y_size, y_size)
        pieces.append(total.astype(BF))
    return jnp.concatenate(pieces, axis=1)


def from_last(feature_all, section_index, section_size):
    for bit in reversed(range(section_size.bit_length() - 1)):
        got = lax.ppermute(feature_all, "section", spread_pairs(section_size, bit))
        takes = (section_index >> bit & 1 == 0) & (
            section_index & ((1 << bit) - 1) == (1 << bit) - 1
        )
        feature_all = jnp.where(takes, got, feature_all)
    return feature_all


def local(
    activations,
    norm_gain,
    trunk_weight,
    head_weight,
    head_mix,
    head_steps,
    task_of,
    loss_ratio,
    targets,
):
    fsdp_size = lax.axis_size("fsdp")
    section_size = lax.axis_size("section")
    member = lax.axis_index("fsdp")
    section_index = lax.axis_index("section")
    last_section = section_size - 1
    is_last = section_index == last_section
    section_bits = section_size.bit_length() - 1
    y_size = 1 << ((fsdp_size.bit_length() - 1) // 2)
    z_size = fsdp_size // y_size
    y_place = member % y_size
    z_place = member // y_size
    tasks, head_rows, outs = head_weight.shape

    hidden = activations[0]
    rows, features = hidden.shape
    weight = trunk_weight[0]
    fused = kernels_fit(rows, features, fsdp_size, section_size, head_rows, tasks)
    wanted = head_weight[task_of[:, 0]]
    if fused:
        pre, output, feature_all, head_w = project(
            hidden, norm_gain, weight, wanted, fsdp_size, section_size
        )
    else:
        normed = (rms_scale(hidden.astype(F32)) * norm_gain[0]).astype(BF)
        feature_block = lax.all_to_all(normed, "fsdp", split_axis=1, concat_axis=0, tiled=True)
        pre = project_permuted(feature_block, weight, rows, y_size, z_size, y_place, z_place)
        feature_all = from_last(feature_block, section_index, section_size)
        part = wanted
        if head_rows % (16 * section_size) == 0:
            share = head_rows // section_size
            part = lax.dynamic_slice_in_dim(part, section_index * share, share, 1)
        part = lax.all_to_all(part, "fsdp", split_axis=0, concat_axis=0, tiled=True)
        if part.shape[1] != head_rows:
            part = lax.all_gather(part, "section", axis=1, tiled=True)
        head_w = part
    head_w = head_w.reshape(features, outs)

    if not fused:
        output = (hidden.astype(F32) + jax.nn.silu(pre.astype(F32))).astype(BF)
        passed = lax.ppermute(output, "section", [(i, i + 1) for i in range(section_size - 1)])

    task_id = task_of[member, 0]
    onehot = (task_of[:, 0][:, None] == jnp.arange(tasks)[None, :]).astype(F32)
    counts = rows * jnp.sum(onehot, axis=0)
    own_task = (jnp.arange(tasks) == task_id).astype(F32)

    def head_pass(output, pre, head_w):
        block_loss, pullback = jax.vjp(
            lambda inner: head_loss(
                inner, head_w, head_mix[task_id], head_steps[task_id] + 1, targets, tasks
            ),
            output.astype(F32),
        )
        grad_out = pullback(jnp.ones_like(block_loss))[0]
        square = jnp.sum(grad_out * grad_out)
        pre_float = pre.astype(F32)
        sigmoid_pre = jax.nn.sigmoid(pre_float)
        slope_term = sigmoid_pre * (1.0 + pre_float * (1.0 - sigmoid_pre))
        cotangent = (grad_out * slope_term).astype(BF)
        return cotangent, jnp.concatenate([own_task * square, own_task * block_loss])

    if fused:
        cotangent, sums = lax.cond(
            is_last,
            head_pass,
            lambda output, pre, head_w: (jnp.zeros_like(output), jnp.zeros((2 * tasks,), F32)),
            output, pre, head_w,
        )
    else:
        cotangent, sums = head_pass(output, pre, head_w)
    col_width = features // section_size
    if fused:
        order = onehot.reshape(z_size, y_size, tasks).swapaxes(0, 1).reshape(fsdp_size, tasks)
        order = jnp.pad(order, ((0, 0), (0, 128 - tasks)))
        order = jnp.broadcast_to(order[:, None, :], (fsdp_size, 8, 128))
        powers = jnp.pad(loss_ratio**ALPHA, (0, 128 - tasks), constant_values=1.0)
        joined_grad, sums, weights, passed = joined_product(
            cotangent,
            jnp.broadcast_to(jnp.pad(sums, (0, 128 - 2 * tasks))[None, :], (8, 128)),
            feature_all,
            order,
            jnp.broadcast_to(powers[None, :], (8, 128)),
            output,
            tasks,
            fsdp_size,
            section_size,
        )
        task_losses = sums[0, tasks : 2 * tasks] / (counts * outs)
        return (passed[None], joined_grad, weights[0, :tasks], task_losses)
    cols = cotangent.reshape(rows, section_size, col_width)
    for bit in reversed(range(section_bits)):
        half = cols.reshape(rows, 2, cols.shape[1] // 2, col_width)
        low, high = half[:, 0], half[:, 1]
        got = lax.ppermute(low, "section", spread_pairs(section_size, bit))
        cols = jnp.where(section_index >> bit & 1 == 0, got, high)
    column_block = lax.all_gather(cols[:, 0], "fsdp", axis=0, tiled=True)
    sums = lax.psum(jnp.where(is_last, sums, jnp.zeros_like(sums)), ("section", "fsdp"))
    norm_sums, loss_sums = sums[:tasks], sums[tasks:]
    grad_norms = jnp.sqrt(norm_sums)
    ratios = jnp.mean(grad_norms) * loss_ratio**ALPHA / grad_norms
    task_weights = tasks * ratios / jnp.sum(ratios)
    task_losses = loss_sums / (counts * outs)

    block_weight = jnp.sum(onehot * task_weights[None, :], axis=1)
    scaled = (
        column_block.reshape(fsdp_size, rows, col_width).astype(F32)
        * block_weight[:, None, None]
    ).astype(BF)
    joined_grad = lax.dot_general(
        feature_all,
        scaled.reshape(fsdp_size * rows, col_width),
        (((0,), (0,)), ((), ())),
        preferred_element_type=F32,
    )
    return (passed[None], joined_grad, task_weights, task_losses)


def solution(mesh):
    return jax.shard_map(
        local,
        mesh=mesh,
        in_specs=(
            P("section", "fsdp", None),
            P("section", None),
            P("section", "fsdp", None),
            P(None, "fsdp", None),
            P(),
            P(),
            P(),
            P(),
            P("fsdp", None),
        ),
        out_specs=(P("section", "fsdp", None), P("fsdp", "section"), P(), P()),
        check_vma=False,
    )
```

```python
import functools

import jax
import jax.numpy as jnp
from jax import lax
from jax.experimental import pallas as pl
from jax.experimental.pallas import tpu as pltpu
from jax.sharding import PartitionSpec as P

EPS = 1e-05
ALPHA = 1.5
BF = jnp.bfloat16
F32 = jnp.float32
MESH = pl.DeviceIdType.MESH
CHUNKS = 8
HALVES = 2
VMEM_MAX = 48 << 20


def rms_scale(values):
    return values * lax.rsqrt(jnp.mean(values * values, axis=-1, keepdims=True) + EPS)


def head_loss(blocks, head_w, mix_w, step_total, target, tasks):
    head_in = rms_scale(blocks).astype(BF)
    outputs = jnp.dot(head_in, head_w, preferred_element_type=F32)
    for depth_index in range(tasks):
        active = (depth_index < step_total).astype(F32)
        outputs = outputs + active * jnp.tanh(
            jnp.dot(outputs, mix_w, precision=lax.Precision.HIGHEST)
        )
    error_term = outputs - target.astype(F32)
    return 0.5 * jnp.sum(error_term * error_term)


def line_reduce_scatter(blocks, place, count, inner, stride):
    if count == 1:
        return blocks[0].astype(F32)
    devices = lax.axis_size("fsdp")

    def pairs(step, limit):
        found = []
        for index in range(devices):
            spot = index // stride % count
            if 0 <= spot + step < count and limit(spot):
                found.append((index, index + step * stride))
        return found

    def pick(position):
        return lax.dynamic_index_in_dim(blocks, jnp.clip(position, 0, count - 1), 0, keepdims=False)

    own = pick(place).astype(F32)
    if count == 2:
        swap = pairs(1, lambda s: True) + pairs(-1, lambda s: True)
        return own + lax.ppermute(pick(1 - place).astype(BF), "fsdp", swap).astype(F32)
    right = left = None
    for t in range(1, count):
        send_right = pick(count - t + place)
        send_left = pick(place - count + t)
        if right is not None:
            send_right = send_right.astype(F32) + right.astype(F32)
            send_left = send_left.astype(F32) + left.astype(F32)
        right = lax.ppermute(send_right.astype(BF), "fsdp", pairs(1, lambda s: s <= t - 1))
        left = lax.ppermute(send_left.astype(BF), "fsdp", pairs(-1, lambda s: s >= count - t))
    return own + right.astype(F32) + left.astype(F32)


def spread_pairs(size, bit):
    low = (1 << (bit + 1)) - 1
    return [(i, i ^ (1 << bit)) for i in range(size) if i & low == low]


def remote(src, dst, send, recv, **place):
    return pltpu.make_async_remote_copy(
        src_ref=src, dst_ref=dst, send_sem=send, recv_sem=recv, device_id=place,
        device_id_type=MESH,
    )


def greet(fsdp, sections):
    me, section = lax.axis_index("fsdp"), lax.axis_index("section")
    barrier = pltpu.get_barrier_semaphore()
    for j in range(1, fsdp):
        pl.semaphore_signal(
            barrier, inc=1, device_id={"fsdp": lax.rem(me + j, fsdp)}, device_id_type=MESH
        )
    for j in range(1, sections):
        pl.semaphore_signal(
            barrier, inc=1, device_id={"section": lax.rem(section + j, sections)},
            device_id_type=MESH,
        )
    pl.semaphore_wait(barrier, fsdp + sections - 2)


def project_kernel(
    fsdp, sections, planes, chunks,
    hidden, gain, weight, wanted, pre, out, feat, head,
    normed, tokens, part, y_in, z_in, z_in0, head_in,
    tok_send, tok_recv, y_send, y_recv, z_send, z_recv, f_send, f_recv,
    h_send, h_recv, hx_send, hx_recv, go,
):
    me, section = lax.axis_index("fsdp"), lax.axis_index("section")
    y, z = lax.rem(me, 2), me // 2
    rows, features = hidden.shape
    depth = features // fsdp
    width = features // chunks
    last = sections - 1
    greet(fsdp, sections)

    @pl.loop(0, rows // 16)
    def _(i):
        r = pl.ds(pl.multiple_of(i * 16, 16), 16)
        normed[r, :] = (rms_scale(hidden[r, :].astype(F32)) * gain[...]).astype(BF)

    def token_copy(lane, j):
        to = lax.rem(z + j, planes) * 2 + (1 - y if lane == 0 else y)
        return remote(
            normed.at[:, pl.ds(pl.multiple_of(to * depth, 128), depth)], tokens.at[y, z],
            tok_send.at[lane, j], tok_recv.at[lane, j], fsdp=to,
        )

    share = head_in.shape[1]

    def head_copy(j):
        to = lax.rem(me + j, fsdp)
        return remote(
            wanted.at[to, pl.ds(pl.multiple_of(section * share, 16), share)], head_in.at[me],
            h_send.at[j - 1], h_recv.at[j - 1], fsdp=to,
        )

    def head_forward(source):
        return remote(
            head_in, head.at[:, source], hx_send, hx_recv.at[source], section=last
        )

    for j in range(planes):
        token_copy(0, j).start()
    tokens[y, z] = normed[:, pl.ds(pl.multiple_of(me * depth, 128), depth)]
    head_in[me] = wanted[me, pl.ds(pl.multiple_of(section * share, 16), share)]
    for j in range(planes):
        token_copy(0, j).wait_send()
    for j in range(1, planes):
        token_copy(1, j).start()
    for j in range(1, fsdp):
        head_copy(j).start()
    def feature_copy(to):
        return remote(tokens, feat, f_send.at[to], f_recv, section=to)

    def y_copy(c):
        return remote(
            part.at[c, 1 - y], y_in.at[c], y_send.at[c], y_recv.at[c], fsdp=z * 2 + 1 - y
        )

    def y_copy0():
        return remote(
            part.at[0, 1 - y, z], y_in.at[0, 0], y_send.at[0], y_recv.at[0], fsdp=z * 2 + 1 - y
        )

    def z_copy(c, way, t):
        d = planes - t + z if way == 0 else z - planes + t
        d = jnp.minimum(jnp.maximum(d, 0), planes - 1)
        to = jnp.minimum(z + 1, planes - 1) if way == 0 else jnp.maximum(z - 1, 0)
        if isinstance(c, int):
            src, dst = part.at[0, :, d], z_in0.at[way, t - 1]
        else:
            src, dst = part.at[c, y, d], z_in.at[c, way, t - 1]
        return d, remote(
            src, dst, z_send.at[c, way, t - 1], z_recv.at[c, way, t - 1], fsdp=to * 2 + y
        )

    def sends(way, t):
        if way == 0:
            return (z <= t - 1) & (z < planes - 1)
        return (z >= planes - t) & (z > 0)

    def receives(way, t):
        if way == 0:
            return (z >= 1) & (z <= t)
        return (z <= planes - 2) & (z >= planes - 1 - t)

    def z_start(c, t):
        for way in range(2):
            d, copy = z_copy(c, way, t)
            if t > 1:

                @pl.when(sends(way, t) & receives(way, t - 1))
                def _():
                    z_copy(c, way, t - 1)[1].wait_recv()
                    if isinstance(c, int):
                        for k in range(2):
                            part[0, k, d] = (
                                part[0, k, d].astype(F32) + z_in0[way, t - 2, k].astype(F32)
                            ).astype(BF)
                    else:
                        part[c, y, d] = (
                            part[c, y, d].astype(F32) + z_in[c, way, t - 2].astype(F32)
                        ).astype(BF)

            @pl.when(sends(way, t))
            def _():
                copy.start()

    def z_last(c):
        t = planes - 1
        for way in range(2):

            @pl.when(receives(way, t))
            def _():
                z_copy(c, way, t)[1].wait_recv()
                if isinstance(c, int):
                    for k in range(2):
                        part[0, k, z] = (
                            part[0, k, z].astype(F32) + z_in0[way, t - 1, k].astype(F32)
                        ).astype(BF)
                else:
                    part[c, y, z] = (
                        part[c, y, z].astype(F32) + z_in[c, way, t - 1].astype(F32)
                    ).astype(BF)

    ahead = min(3, chunks - 1)

    def multiply(c, lane):
        block = weight[:, pl.ds(pl.multiple_of(c * width, 128), width)]
        part[c, lane] = (
            jnp.dot(tokens[lane].reshape(planes * rows, depth), block, preferred_element_type=F32)
            .astype(BF)
            .reshape(planes, rows, width)
        )

    def finish(c, value):
        columns = pl.ds(pl.multiple_of(c * width, 128), width)
        pre[:, columns] = value
        wide = value.astype(F32)
        out[:, columns] = (
            hidden[:, columns].astype(F32) + wide * jax.nn.sigmoid(wide)
        ).astype(BF)

    beside = last - 1

    for j in range(planes):
        token_copy(0, j).wait_recv()
        d = lax.rem(z + planes - j, planes)

        @pl.loop(1, ahead + 1)
        def _(c):
            block = weight[:, pl.ds(pl.multiple_of(c * width, 128), width)]
            part[c, 1 - y, d] = jnp.dot(
                tokens[1 - y, d], block, preferred_element_type=F32
            ).astype(BF)

            @pl.when(section != beside)
            def _():
                remote(
                    part.at[c, 1 - y, d], y_in.at[c, d], y_send.at[c], y_recv.at[c],
                    fsdp=z * 2 + 1 - y,
                ).start()

    for j in range(1, planes):
        token_copy(1, j).wait_recv()

    @pl.when(section == last)
    def _():
        for to in range(last):
            feature_copy(to).start()
        feat[...] = tokens[...]

    multiply(0, 1 - y)
    multiply(0, y)

    @pl.when(section != beside)
    def _():
        z_start(0, 1)

    multiply(1, y)

    def share_head():
        for j in range(1, fsdp):
            head_copy(j).wait_recv()

        @pl.when(section != last)
        def _():
            head_forward(section).start()

        @pl.when(section == last)
        def _():
            for f in range(fsdp):
                head[f, last] = head_in[f]

    @pl.when(section == beside)
    def _():
        share_head()
        pl.semaphore_wait(go, 1)
        for i in range(1, ahead + 1):
            y_copy(i).start()
        z_start(0, 1)

    @pl.loop(1, chunks + planes - 1)
    def _(i):
        @pl.when(i + ahead < chunks)
        def _():
            multiply(i + ahead, 1 - y)

        @pl.when(i < chunks)
        def _():
            y_copy(i).wait_recv()

            @pl.when(i + ahead < chunks)
            def _():
                y_copy(i + ahead).start()

            @pl.when((i == chunks - 2) & (section == last))
            def _():
                pl.semaphore_signal(
                    go, inc=1, device_id={"section": beside}, device_id_type=MESH
                )

            for d in range(planes):
                part[i, y, d] = (part[i, y, d].astype(F32) + y_in[i, d].astype(F32)).astype(BF)
            z_start(i, 1)

        for t in range(1, planes - 1):
            c = i - t

            @pl.when((c >= 1) & (c < chunks))
            def _():
                z_start(c, t + 1)

        c = i - (planes - 1)

        @pl.when((c >= 1) & (c < chunks))
        def _():
            z_last(c)
            finish(c, part[c, y, z])

        for t in range(1, planes):

            @pl.when(i == t)
            def _():
                if t < planes - 1:
                    z_start(0, t + 1)
                else:
                    z_last(0)
                    y_copy0().start()

        @pl.when((i == 2) & (section != beside))
        def _():
            share_head()

        @pl.when(i + 1 < chunks)
        def _():
            multiply(i + 1, y)

    y_copy0().wait_recv()
    finish(0, (part[0, y, z].astype(F32) + y_in[0, 0].astype(F32)).astype(BF))

    @pl.when(section != last)
    def _():
        feature_copy(0).wait_recv()

    @pl.when(section == last)
    def _():
        for to in range(last):
            feature_copy(to).wait_send()

    @pl.when(section != last)
    def _():
        head[...] = jnp.zeros_like(head)
        head_forward(section).wait_send()

    @pl.when(section == last)
    def _():
        for source in range(last):
            head_forward(source).wait_recv()

    for j in range(1, planes):
        token_copy(1, j).wait_send()
    for j in range(1, fsdp):
        head_copy(j).wait_send()
    y_copy0().wait_send()
    for t in range(1, planes):
        for way in range(2):

            @pl.when(sends(way, t))
            def _():
                z_copy(0, way, t)[1].wait_send()

    @pl.loop(1, chunks)
    def _(c):
        y_copy(c).wait_send()
        for t in range(1, planes):
            for way in range(2):

                @pl.when(sends(way, t))
                def _():
                    z_copy(c, way, t)[1].wait_send()


def project(hidden, gain, weight, wanted, fsdp, sections):
    rows, features = hidden.shape
    share, outs = wanted.shape[1] // sections, wanted.shape[2]
    planes, chunks = fsdp // 2, CHUNKS
    depth, width = features // fsdp, features // chunks
    dma = pltpu.SemaphoreType.DMA
    vmem = pl.BlockSpec(memory_space=pltpu.VMEM)
    return pl.pallas_call(
        functools.partial(project_kernel, fsdp, sections, planes, chunks),
        out_shape=(
            jax.ShapeDtypeStruct((rows, features), BF),
            jax.ShapeDtypeStruct((rows, features), BF),
            jax.ShapeDtypeStruct((2, planes, rows, depth), BF),
            jax.ShapeDtypeStruct((fsdp, sections, share, outs), BF),
        ),
        in_specs=[vmem] * 4,
        out_specs=(vmem,) * 4,
        scratch_shapes=[
            pltpu.VMEM((rows, features), BF),
            pltpu.VMEM((2, planes, rows, depth), BF),
            pltpu.VMEM((chunks, 2, planes, rows, width), BF),
            pltpu.VMEM((chunks, planes, rows, width), BF),
            pltpu.VMEM((chunks, 2, planes - 1, rows, width), BF),
            pltpu.VMEM((2, planes - 1, 2, rows, width), BF),
            pltpu.VMEM((fsdp, share, outs), BF),
            dma((2, planes)),
            dma((2, planes)),
            dma((chunks,)),
            dma((chunks,)),
            dma((chunks, 2, planes - 1)),
            dma((chunks, 2, planes - 1)),
            dma((sections,)),
            dma,
            dma((fsdp - 1,)),
            dma((fsdp - 1,)),
            dma,
            dma((sections,)),
            pltpu.SemaphoreType.REGULAR,
        ],
        compiler_params=pltpu.CompilerParams(
            collective_id=0, has_side_effects=True, vmem_limit_bytes=VMEM_MAX
        ),
        cost_estimate=pl.CostEstimate(
            flops=2 * fsdp * rows * depth * features, bytes_accessed=1 << 23, transcendentals=0
        ),
    )(hidden, gain, weight, wanted)


def gather_kernel(
    fsdp, sections, planes,
    tasks, cot, stats, feat, order, powers, out, joined, sums, weights, passed, cols, table,
    x_send, x_recv, sx_send, sx_recv, st_send, st_recv, z_send, z_recv, y_send, y_recv,
    p_send, p_recv,
):
    me, section = lax.axis_index("fsdp"), lax.axis_index("section")
    y, z = lax.rem(me, 2), me // 2
    last = sections - 1
    rows, features = cot.shape
    width = features // sections
    size = rows // HALVES
    greet(fsdp, sections)

    def pass_copy():
        return remote(out, passed, p_send, p_recv, section=lax.rem(section + 1, sections))

    def stats_x(to):
        return remote(stats, table.at[y, z], sx_send.at[to], sx_recv, section=to)

    def cols_x(to, h):
        return remote(
            cot.at[pl.ds(h * size, size), pl.ds(to * width, width)], cols.at[y, z, h],
            x_send.at[to, h], x_recv.at[h], section=to,
        )

    def stats_f(j):
        return remote(
            table.at[y, z], table.at[y, z], st_send.at[j - 1], st_recv.at[j - 1],
            fsdp=lax.rem(me + j, fsdp),
        )

    def y_copy(plane, h):
        block = cols.at[y, plane, h]
        return remote(
            block, block, y_send.at[plane, h], y_recv.at[plane, h], fsdp=z * 2 + 1 - y
        )

    def z_copy(way, t, h):
        if way == 0:
            plane, to = jnp.maximum(z - t + 1, 0), jnp.minimum(z + 1, planes - 1)
        else:
            plane, to = jnp.minimum(z + t - 1, planes - 1), jnp.maximum(z - 1, 0)
        block = cols.at[y, plane, h]
        return remote(
            block, block, z_send.at[way, t - 1, h], z_recv.at[way, t - 1, h], fsdp=to * 2 + y
        )

    def sends(way, t):
        if way == 0:
            return (z < planes - 1) & (z - t + 1 >= 0)
        return (z > 0) & (z + t - 1 <= planes - 1)

    def receives(way, t):
        return z - t >= 0 if way == 0 else z + t <= planes - 1

    @pl.when(section == last)
    def _():
        for to in range(last):
            stats_x(to).start()
        for h in range(HALVES):
            for to in range(last):
                cols_x(to, h).start()
        table[y, z] = stats[...]
        for h in range(HALVES):
            cols[y, z, h] = cot[pl.ds(h * size, size), pl.ds(last * width, width)]

    @pl.when(section != last)
    def _():
        stats_x(0).wait_recv()

    for j in range(1, fsdp):
        stats_f(j).start()

    @pl.when(section != last)
    def _():
        pass_copy().start()

    @pl.when(section == 0)
    def _():
        passed[...] = jnp.zeros_like(passed)

    def add(lane, plane):
        block = cols[lane, plane].reshape(rows, width).astype(F32)
        row = order[pl.ds(lane * planes + plane, 1)][0]
        scale = jnp.sum(row * weights[...], axis=1, keepdims=True)[:1]
        block = (block * scale).astype(BF)
        joined[...] += lax.dot_general(
            feat[lane, plane], block, (((0,), (0,)), ((), ())), preferred_element_type=F32
        )

    def add_across(plane):
        for h in range(HALVES):
            y_copy(plane, h).wait_recv()
        add(1 - y, plane)

    joined[...] = jnp.zeros_like(joined)
    for h in range(HALVES):

        @pl.when(section != last)
        def _():
            cols_x(0, h).wait_recv()

        for way in range(2):

            @pl.when(sends(way, 1))
            def _():
                z_copy(way, 1, h).start()

        y_copy(z, h).start()
    for j in range(1, fsdp):
        stats_f(j).wait()
    total = jnp.sum(table[...], axis=(0, 1))
    sums[...] = total
    lane_number = lax.broadcasted_iota(jnp.int32, total.shape, 1)
    counted = lane_number < tasks
    norms = jnp.sqrt(total)
    mean_norm = jnp.sum(jnp.where(counted, norms, 0.0), axis=1, keepdims=True) / tasks
    ratios = jnp.where(counted, mean_norm * powers[...] / norms, 0.0)
    weights[...] = tasks * ratios / jnp.sum(ratios, axis=1, keepdims=True)

    for t in range(1, planes):
        for h in range(HALVES):
            for way in range(2):

                @pl.when(receives(way, t))
                def _():
                    z_copy(way, t, h).wait_recv()
                    y_copy(z - t if way == 0 else z + t, h).start()

                if t < planes - 1:

                    @pl.when(sends(way, t + 1))
                    def _():
                        z_copy(way, t + 1, h).start()

        if t == 1:
            add(y, z)
            add_across(z)
        for way in range(2):

            @pl.when(receives(way, t))
            def _():
                add(y, z - t if way == 0 else z + t)

            if t > 1:

                @pl.when(receives(way, t - 1))
                def _():
                    add_across(z - t + 1 if way == 0 else z + t - 1)

    for way in range(2):

        @pl.when(receives(way, planes - 1))
        def _():
            add_across(z - planes + 1 if way == 0 else z + planes - 1)

    @pl.when(section != 0)
    def _():
        pass_copy().wait_recv()

    @pl.when(section != last)
    def _():
        pass_copy().wait_send()

    for plane in range(planes):
        for h in range(HALVES):
            y_copy(plane, h).wait_send()
    for t in range(1, planes):
        for h in range(HALVES):
            for way in range(2):

                @pl.when(sends(way, t))
                def _():
                    z_copy(way, t, h).wait_send()

    @pl.when(section == last)
    def _():
        for to in range(last):
            stats_x(to).wait_send()
            for h in range(HALVES):
                cols_x(to, h).wait_send()


def joined_product(cot, stats, feat, order, powers, out, tasks, fsdp, sections):
    rows, features = cot.shape
    planes = fsdp // 2
    width = features // sections
    dma = pltpu.SemaphoreType.DMA
    vmem = pl.BlockSpec(memory_space=pltpu.VMEM)
    return pl.pallas_call(
        functools.partial(gather_kernel, fsdp, sections, planes, tasks),
        out_shape=(
            jax.ShapeDtypeStruct((feat.shape[3], width), F32),
            jax.ShapeDtypeStruct(stats.shape, F32),
            jax.ShapeDtypeStruct(stats.shape, F32),
            jax.ShapeDtypeStruct(out.shape, BF),
        ),
        in_specs=[vmem] * 6,
        out_specs=(vmem,) * 4,
        scratch_shapes=[
            pltpu.VMEM((2, planes, HALVES, rows // HALVES, width), BF),
            pltpu.VMEM((2, planes) + stats.shape, F32),
            dma((sections, HALVES)),
            dma((HALVES,)),
            dma((sections,)),
            dma,
            dma((fsdp - 1,)),
            dma((fsdp - 1,)),
            dma((2, planes - 1, HALVES)),
            dma((2, planes - 1, HALVES)),
            dma((planes, HALVES)),
            dma((planes, HALVES)),
            dma,
            dma,
        ],
        compiler_params=pltpu.CompilerParams(
            collective_id=1, has_side_effects=True, vmem_limit_bytes=VMEM_MAX
        ),
        cost_estimate=pl.CostEstimate(flops=0, bytes_accessed=1 << 23, transcendentals=0),
    )(cot, stats, feat, order, powers, out)


def kernels_fit(rows, features, fsdp, sections, head_rows, tasks):
    if fsdp < 4 or fsdp % 2 or sections < 2:
        return False
    planes = fsdp // 2
    block = rows * features * 2
    planned = block * (2 * planes + planes + 2 * planes - 2 + 10) + features // fsdp * features * 2
    return (
        planned <= VMEM_MAX * 3 // 4
        and rows % (16 * HALVES) == 0
        and CHUNKS >= planes + 1
        and features % (128 * CHUNKS) == 0
        and features % (128 * fsdp) == 0
        and features % (128 * sections) == 0
        and head_rows % (16 * sections) == 0
        and 2 * tasks <= 128
        and 1 << ((fsdp.bit_length() - 1) // 2) == 2
    )


def project_permuted(feature_block, weight, rows, y_size, z_size, y_place, z_place):
    features = weight.shape[1]
    chunks = 4
    width = features // chunks
    pieces = []
    for c in range(chunks):
        partial = jnp.dot(
            feature_block, weight[:, c * width : (c + 1) * width], preferred_element_type=F32
        ).astype(BF)
        partial = partial.reshape(z_size, y_size, rows, width)
        if c == 1:
            partial = line_reduce_scatter(partial, z_place, z_size, y_size, y_size)
            total = line_reduce_scatter(partial, y_place, y_size, 1, 1)
        else:
            partial = line_reduce_scatter(partial.swapaxes(0, 1), y_place, y_size, 1, 1)
            total = line_reduce_scatter(partial, z_place, z_size, y_size, y_size)
        pieces.append(total.astype(BF))
    return jnp.concatenate(pieces, axis=1)


def from_last(feature_all, section_index, section_size):
    for bit in reversed(range(section_size.bit_length() - 1)):
        got = lax.ppermute(feature_all, "section", spread_pairs(section_size, bit))
        takes = (section_index >> bit & 1 == 0) & (
            section_index & ((1 << bit) - 1) == (1 << bit) - 1
        )
        feature_all = jnp.where(takes, got, feature_all)
    return feature_all


def local(
    activations,
    norm_gain,
    trunk_weight,
    head_weight,
    head_mix,
    head_steps,
    task_of,
    loss_ratio,
    targets,
):
    fsdp_size = lax.axis_size("fsdp")
    section_size = lax.axis_size("section")
    member = lax.axis_index("fsdp")
    section_index = lax.axis_index("section")
    last_section = section_size - 1
    is_last = section_index == last_section
    section_bits = section_size.bit_length() - 1
    y_size = 1 << ((fsdp_size.bit_length() - 1) // 2)
    z_size = fsdp_size // y_size
    y_place = member % y_size
    z_place = member // y_size
    tasks, head_rows, outs = head_weight.shape

    hidden = activations[0]
    rows, features = hidden.shape
    weight = trunk_weight[0]
    fused = kernels_fit(rows, features, fsdp_size, section_size, head_rows, tasks)
    wanted = head_weight[task_of[:, 0]]
    if fused:
        pre, output, feature_all, head_w = project(
            hidden, norm_gain, weight, wanted, fsdp_size, section_size
        )
    else:
        normed = (rms_scale(hidden.astype(F32)) * norm_gain[0]).astype(BF)
        feature_block = lax.all_to_all(normed, "fsdp", split_axis=1, concat_axis=0, tiled=True)
        pre = project_permuted(feature_block, weight, rows, y_size, z_size, y_place, z_place)
        feature_all = from_last(feature_block, section_index, section_size)
        part = wanted
        if head_rows % (16 * section_size) == 0:
            share = head_rows // section_size
            part = lax.dynamic_slice_in_dim(part, section_index * share, share, 1)
        part = lax.all_to_all(part, "fsdp", split_axis=0, concat_axis=0, tiled=True)
        if part.shape[1] != head_rows:
            part = lax.all_gather(part, "section", axis=1, tiled=True)
        head_w = part
    head_w = head_w.reshape(features, outs)

    if not fused:
        output = (hidden.astype(F32) + jax.nn.silu(pre.astype(F32))).astype(BF)
        passed = lax.ppermute(output, "section", [(i, i + 1) for i in range(section_size - 1)])

    task_id = task_of[member, 0]
    onehot = (task_of[:, 0][:, None] == jnp.arange(tasks)[None, :]).astype(F32)
    counts = rows * jnp.sum(onehot, axis=0)
    own_task = (jnp.arange(tasks) == task_id).astype(F32)

    def head_pass(output, pre, head_w):
        block_loss, pullback = jax.vjp(
            lambda inner: head_loss(
                inner, head_w, head_mix[task_id], head_steps[task_id] + 1, targets, tasks
            ),
            output.astype(F32),
        )
        grad_out = pullback(jnp.ones_like(block_loss))[0]
        square = jnp.sum(grad_out * grad_out)
        pre_float = pre.astype(F32)
        sigmoid_pre = jax.nn.sigmoid(pre_float)
        slope_term = sigmoid_pre * (1.0 + pre_float * (1.0 - sigmoid_pre))
        cotangent = (grad_out * slope_term).astype(BF)
        return cotangent, jnp.concatenate([own_task * square, own_task * block_loss])

    if fused:
        cotangent, sums = lax.cond(
            is_last,
            head_pass,
            lambda output, pre, head_w: (jnp.zeros_like(output), jnp.zeros((2 * tasks,), F32)),
            output, pre, head_w,
        )
    else:
        cotangent, sums = head_pass(output, pre, head_w)
    col_width = features // section_size
    if fused:
        order = onehot.reshape(z_size, y_size, tasks).swapaxes(0, 1).reshape(fsdp_size, tasks)
        order = jnp.pad(order, ((0, 0), (0, 128 - tasks)))
        order = jnp.broadcast_to(order[:, None, :], (fsdp_size, 8, 128))
        powers = jnp.pad(loss_ratio**ALPHA, (0, 128 - tasks), constant_values=1.0)
        joined_grad, sums, weights, passed = joined_product(
            cotangent,
            jnp.broadcast_to(jnp.pad(sums, (0, 128 - 2 * tasks))[None, :], (8, 128)),
            feature_all,
            order,
            jnp.broadcast_to(powers[None, :], (8, 128)),
            output,
            tasks,
            fsdp_size,
            section_size,
        )
        task_losses = sums[0, tasks : 2 * tasks] / (counts * outs)
        return (passed[None], joined_grad, weights[0, :tasks], task_losses)
    cols = cotangent.reshape(rows, section_size, col_width)
    for bit in reversed(range(section_bits)):
        half = cols.reshape(rows, 2, cols.shape[1] // 2, col_width)
        low, high = half[:, 0], half[:, 1]
        got = lax.ppermute(low, "section", spread_pairs(section_size, bit))
        cols = jnp.where(section_index >> bit & 1 == 0, got, high)
    column_block = lax.all_gather(cols[:, 0], "fsdp", axis=0, tiled=True)
    sums = lax.psum(jnp.where(is_last, sums, jnp.zeros_like(sums)), ("section", "fsdp"))
    norm_sums, loss_sums = sums[:tasks], sums[tasks:]
    grad_norms = jnp.sqrt(norm_sums)
    ratios = jnp.mean(grad_norms) * loss_ratio**ALPHA / grad_norms
    task_weights = tasks * ratios / jnp.sum(ratios)
    task_losses = loss_sums / (counts * outs)

    block_weight = jnp.sum(onehot * task_weights[None, :], axis=1)
    scaled = (
        column_block.reshape(fsdp_size, rows, col_width).astype(F32)
        * block_weight[:, None, None]
    ).astype(BF)
    joined_grad = lax.dot_general(
        feature_all,
        scaled.reshape(fsdp_size * rows, col_width),
        (((0,), (0,)), ((), ())),
        preferred_element_type=F32,
    )
    return (passed[None], joined_grad, task_weights, task_losses)


def solution(mesh):
    return jax.shard_map(
        local,
        mesh=mesh,
        in_specs=(
            P("section", "fsdp", None),
            P("section", None),
            P("section", "fsdp", None),
            P(None, "fsdp", None),
            P(),
            P(),
            P(),
            P(),
            P("fsdp", None),
        ),
        out_specs=(P("section", "fsdp", None), P("fsdp", "section"), P(), P()),
        check_vma=False,
    )
```
